128 devices in a mesh: row: 32 (over z, x, core), col: 4 (over y).
Axes of the slice: x: 4, y: 4, z: 4, core: 2. Of those that a mesh axis runs over, the one named last changes fastest.
Arguments:
- features: bfloat16 [32768, 256], P(('col', 'row')), may hold values from -6 to 6
- cotangent: bfloat16 [32768, 256], P(('row', 'col')), may hold values from -6 to 6
- weight: bfloat16 [256, 256], replicated, may hold values from -0.375 to 0.375
- tile_values: bfloat16 [32, 4, 384, 128, 128], P('row', 'col'), may hold values from 0 to 0.011962891
- tile_rows: int32 [32, 4, 384], P('row', 'col'), may hold values from 0 to 7, as said below
- tile_cols: int32 [32, 4, 384], P('row', 'col'), may hold values from 0 to 63, as said below
- tile_count: int32 [32, 4], P('row', 'col'), may hold values from 128 to 384, as said below
Outputs:
- activated: bfloat16 [32768, 256], P(('row', 'col'))
- weight_grad: float32 [256, 256], replicated
- feature_grad: bfloat16 [32768, 256], P(('col', 'row'))
The draws below stay inside these ranges and needn't reach their ends.
Inputs may be any that keep to these rules, and one draw needn't show every extreme that they name: On each device the first tile_count entries, with tile_cols, name distinct tiles in increasing order of tile_rows * 64 + tile_cols; all entries of a device are distinct tiles. `tile_cols`: see tile_rows. `tile_count`: some device has 384 nonzero tiles.
All inputs are finite; a program needn't handle non-finite values.
Results may differ from the reference program's by a relative error of at most 0.0065.
Values may be sent and summed in bfloat16 or wider, within the bound.
No kernel may reach another device: no remote copies, remote signals or barrier semaphores. Data moves between devices by JAX's collectives and lax.ppermute only.
A program may use at most 192 MiB of HBM per device.

```python
import jax
import jax.numpy as jnp
from jax import lax

FEAT = 256
TILE = 128
ROWS_DEV = 256
NODES = 32768
RB = 8
CB = 64
TILE_CAP = 384
N_ROW = 32
N_COL = 4


def tile_layout(key):
    devices = N_ROW * N_COL
    slots = RB * CB
    key_count, key_top, key_low, key_perm = jax.random.split(key, 4)
    counts = jax.random.randint(key_count, (devices,), TILE_CAP // 3, TILE_CAP + 1)
    top = jax.random.randint(key_top, (), 0, devices)
    low = (top + 1 + jax.random.randint(key_low, (), 0, devices - 1)) % devices
    device_ids = jnp.arange(devices, dtype=jnp.int32)
    counts = jnp.where(device_ids == top, TILE_CAP, counts)
    counts = jnp.where(device_ids == low, TILE_CAP // 3, counts)
    perm_keys = jax.random.split(key_perm, devices)
    perms = jax.vmap(lambda k: jax.random.permutation(k, slots))(perm_keys).astype(jnp.int32)
    slot_ids = jnp.arange(slots, dtype=jnp.int32)[None, :]
    score = jnp.where(slot_ids == 0, -2, jnp.where(slot_ids == slots - 1, -1, perms))
    order = jnp.argsort(score, axis=1, stable=True)
    ranks = jnp.argsort(order, axis=1, stable=True)
    chosen = ranks < counts[:, None]
    sorter = jnp.where(chosen, slot_ids, slot_ids + slots)
    picked = jnp.argsort(sorter, axis=1, stable=True)[:, :TILE_CAP].astype(jnp.int32)
    rows_out = (picked // CB).reshape(N_ROW, N_COL, TILE_CAP)
    cols_out = (picked % CB).reshape(N_ROW, N_COL, TILE_CAP)
    return (rows_out, cols_out, counts.reshape(N_ROW, N_COL).astype(jnp.int32))


def draw_tile_rows(key, part):
    return tile_layout(key)[0]


def draw_tile_cols(key, part):
    return tile_layout(key)[1]


def draw_tile_count(key, part):
    return tile_layout(key)[2]


def levels(rng, dims, cuts, low, high):
    gain, own = 1.0, jax.random.fold_in(rng, 6)
    for position, shards_of in cuts:
        steps = jnp.exp(jax.random.uniform(jax.random.fold_in(own, position), (shards_of,), jnp.float32, low / len(cuts), high / len(cuts)))
        gain = gain * jnp.repeat(steps, dims[position] // shards_of).reshape([-1 if axis == position else 1 for axis in range(len(dims))])
    return gain


def centred(stream_key, dims, spread, limit, cuts=(), held_as=jnp.bfloat16):
    level = levels(stream_key, dims, cuts, -0.22, 0.18) if cuts else 1.0
    drawn = jax.random.normal(stream_key, dims, jnp.float32) * spread * level
    return jnp.minimum(jnp.maximum(drawn, -limit), limit).astype(held_as)


def setup_inputs(seed: int = 0) -> dict:
    streams_of = jax.random.split(jax.random.key(seed), 8)
    features = centred(streams_of[0], (NODES, FEAT), 1.0, 6.0, ((0, 128),))
    cotangent = centred(streams_of[1], (NODES, FEAT), 1.0, 6.0, ((0, 128),))
    weight = centred(streams_of[2], (FEAT, FEAT), FEAT ** -0.5, 0.375)
    tile_values = jnp.clip(0.011962891 * jax.random.uniform(streams_of[3], (N_ROW, N_COL, TILE_CAP, TILE, TILE), jnp.float32) ** levels(streams_of[3], (N_ROW, N_COL, TILE_CAP, TILE, TILE), ((0, 32), (1, 4)), -0.2, 0.2), 0.0, 0.011962891).astype(jnp.bfloat16)
    tile_rows = draw_tile_rows(jax.random.fold_in(streams_of[7], 71), 0)
    tile_cols = draw_tile_cols(jax.random.fold_in(streams_of[7], 71), 0)
    tile_count = draw_tile_count(jax.random.fold_in(streams_of[7], 71), 0)
    return {"features": features, "cotangent": cotangent, "weight": weight, "tile_values": tile_values, "tile_rows": tile_rows, "tile_cols": tile_cols, "tile_count": tile_count}


block_turns = 12


def block_sum(values, rows_idx, cols_idx, count, source, out_blocks, forward):
    cap, tile = values.shape[0], values.shape[1]
    feat = source.shape[1]
    blocks = source.reshape(-1, tile, feat)
    width = cap // block_turns
    slots = jnp.arange(cap, dtype=jnp.int32)
    xs = (values.reshape(block_turns, width, tile, tile), rows_idx.reshape(block_turns, width),
          cols_idx.reshape(block_turns, width), slots.reshape(block_turns, width))

    def step(total, item):
        vals, rws, cls, slt = item
        live = (slt < count).astype(jnp.float32)
        if forward:
            picked = blocks[cls]
            prod = jnp.einsum("bij,bjf->bif", vals.astype(jnp.float32), picked.astype(jnp.float32))
            target = rws
        else:
            picked = blocks[rws]
            prod = jnp.einsum("bji,bjf->bif", vals.astype(jnp.float32), picked.astype(jnp.float32))
            target = cls
        prod = prod * live[:, None, None]
        return total.at[target].add(prod), None

    start = jnp.zeros((out_blocks, tile, feat), jnp.float32)
    total, _ = lax.scan(step, start, xs)
    return total.reshape(out_blocks * tile, feat)


def reference(features, cotangent, weight, tile_values, tile_rows, tile_cols, tile_count):
    bands_in = features.reshape(N_COL, CB * TILE, FEAT)

    def forward_dev(index, total):
        rpos = index // N_COL
        cpos = index % N_COL
        part = block_sum(tile_values[rpos, cpos], tile_rows[rpos, cpos], tile_cols[rpos, cpos],
                         tile_count[rpos, cpos], bands_in[cpos], RB, True)
        return total.at[rpos].add(part)

    summed = lax.fori_loop(0, N_ROW * N_COL, forward_dev, jnp.zeros((N_ROW, RB * TILE, FEAT), jnp.float32))
    agg = summed.reshape(NODES, FEAT).astype(jnp.bfloat16)
    pre = jnp.dot(agg, weight, preferred_element_type=jnp.float32)
    sigma = jax.nn.sigmoid(pre)
    activated = (pre * sigma).astype(jnp.bfloat16)
    dz = (cotangent.astype(jnp.float32) * sigma * (1.0 + pre * (1.0 - sigma))).astype(jnp.bfloat16)
    weight_grad = jnp.dot(agg.T, dz, preferred_element_type=jnp.float32) / ROWS_DEV
    back = jnp.dot(dz, weight.T, preferred_element_type=jnp.float32).astype(jnp.bfloat16)
    back_bands = back.reshape(N_ROW, RB * TILE, FEAT)

    def backward_dev(index, total):
        rpos = index // N_COL
        cpos = index % N_COL
        part = block_sum(tile_values[rpos, cpos], tile_rows[rpos, cpos], tile_cols[rpos, cpos],
                         tile_count[rpos, cpos], back_bands[rpos], CB, False)
        return total.at[cpos].add(part)

    gsum = lax.fori_loop(0, N_ROW * N_COL, backward_dev, jnp.zeros((N_COL, CB * TILE, FEAT), jnp.float32))
    feature_grad = gsum.reshape(NODES, FEAT).astype(jnp.bfloat16)
    return activated, weight_grad, feature_grad
```

```python
import functools

import jax
import jax.numpy as jnp
from jax import lax
from jax.experimental import pallas as pl
from jax.experimental.pallas import tpu as pltpu
from jax.sharding import Mesh
from jax.sharding import PartitionSpec as P

F32 = jnp.float32
BF16 = jnp.bfloat16
TILE = 128
FEAT = 256
NODE = 256
HALF = 128
ROWS = 1024
NCT = 64
CAP = 384
MIB = 1 << 20
PZ, PX, PC, PY = 0, 1, 2, 3


def shape(s, dt):
    return jax.ShapeDtypeStruct(s, dt)


VSPEC = pl.BlockSpec(memory_space=pltpu.VMEM)
SSPEC = pl.BlockSpec(memory_space=pltpu.SMEM)
ASPEC = pl.BlockSpec(memory_space=pl.ANY)


def in_vmem(x):
    return pltpu.with_memory_space_constraint(x, pltpu.VMEM)


def call(kernel, outs, in_specs, scratch=(), flops=0, nbytes=0, limit=16, aliases=None):
    return pl.pallas_call(
        kernel,
        out_shape=outs,
        in_specs=in_specs,
        out_specs=jax.tree.map(lambda _: VSPEC, outs),
        scratch_shapes=list(scratch),
        input_output_aliases=aliases or {},
        cost_estimate=pl.CostEstimate(flops=flops, bytes_accessed=nbytes, transcendentals=0),
        compiler_params=pltpu.CompilerParams(vmem_limit_bytes=limit * MIB),
    )


def place_tiles(lo, hi, tv, rows, cols, dense, sem):
    def copy(s):
        return pltpu.make_async_copy(
            tv.at[s],
            dense.at[cols[s], pl.ds(pl.multiple_of(rows[s] * TILE, TILE), TILE), :],
            sem,
        )

    def start(s, _):
        copy(s).start()
        return 0

    def wait(s, _):
        copy(s).wait()
        return 0

    lax.fori_loop(lo, hi, start, 0)
    lax.fori_loop(lo, hi, wait, 0)


def dense_first(part, tv, rows, cols, count, dense, sem):
    @pl.loop(0, NCT)
    def _(c):
        dense[c] = jnp.zeros((ROWS, TILE), BF16)

    place_tiles(0, jnp.minimum(count[0], part), tv, rows, cols, dense, sem)


def dense_rest(part, tv, rows, cols, count, given, dense, sem):
    del given
    place_tiles(jnp.minimum(count[0], part), count[0], tv, rows, cols, dense, sem)


def columns(dense, z, x, core, dz, dx):
    b = lax.rem(z + dz, 4) * 8 + lax.rem(x + dx, 4) * 2 + core
    return dense[2 * b], dense[2 * b + 1]


def forward_sum(dense, near, far, z, x, core, acc, add):
    for dz in range(4):
        lhs, rhs = [], []
        for dx in range(4):
            lhs += columns(dense, z, x, core, dz, dx)
            if dz == 0:
                rhs.append(near[dx * NODE : (dx + 1) * NODE])
            elif dx == 0:
                rhs.append(near[(3 + dz) * NODE : (4 + dz) * NODE])
            else:
                i = (dz - 1) * 384 + (dx - 1) * HALF
                j = 1152 + (dx - 1) * 384 + (dz - 1) * HALF
                rhs += [far[i : i + HALF], far[j : j + HALF]]
        term = jnp.dot(
            jnp.concatenate(lhs, axis=1),
            jnp.concatenate(rhs, axis=0),
            preferred_element_type=F32,
        )
        if dz == 0 and not add:
            acc[...] = term
        else:
            acc[...] += term


def forward_own(pos, dense, near, far, acc):
    forward_sum(dense, near, far, pos[PZ], pos[PX], pos[PC], acc, False)


def forward_other(pos, dense, near, far, given, own, s1, s2, s3, acc):
    acc[...] = given[...]
    forward_sum(dense, near, far, pos[PZ], pos[PX], 1 - pos[PC], acc, True)
    y = pos[PY]
    for d, out in enumerate((own, s1, s2, s3)):
        row = pl.multiple_of(lax.rem(y + d, 4) * NODE, NODE)
        out[...] = acc[pl.ds(row, NODE), :].astype(out.dtype)


def middle(pos, own, r1, r2, r3, w, cot, act, bt, q, m1, m2, m3, lg):
    agg = (own[...] + r1[...].astype(F32) + r2[...].astype(F32) + r3[...].astype(F32)).astype(BF16)
    pre = jnp.dot(agg, w[...], preferred_element_type=F32)
    sg = jax.nn.sigmoid(pre)
    act[...] = (pre * sg).astype(BF16)
    dz = (cot[...].astype(F32) * sg * (1.0 + pre * (1.0 - sg))).astype(BF16)
    back = lax.dot_general(w[...], dz, (((1,), (1,)), ((), ())), preferred_element_type=F32).astype(
        BF16
    )
    lg[...] = lax.dot_general(agg, dz, (((0,), (0,)), ((), ())), preferred_element_type=F32)
    bt[...] = back
    y = pos[PY]
    for d, out in enumerate((q, m1, m2, m3)):
        row = pl.multiple_of(lax.rem(y + d, 4) * 64, 64)
        piece = lg[pl.ds(row, 64), :]
        if d == 0:
            out[...] = piece
        else:
            out[:NODE] = back
            out[NODE:] = piece.astype(BF16)


def back_all(bt):
    return jnp.concatenate([bt[0], bt[1], bt[2], bt[3]], axis=1)


def backward_block(dense, lhs, z, x, core, dz, dx):
    rhs = jnp.concatenate(columns(dense, z, x, core, dz, dx), axis=1)
    return jnp.dot(lhs, rhs, preferred_element_type=F32)


def backward_other(pos, dense, own, r1, r2, r3, q, out, bt, qown, qsum):
    z, x, core, y = pos[PZ], pos[PX], pos[PC], pos[PY]
    bt[y] = own[...]
    total = q[...]
    for d, r in ((1, r1), (2, r2), (3, r3)):
        bt[lax.rem(y + 4 - d, 4)] = r[:NODE]
        total += r[NODE:].astype(F32)
    qsum[...] = total
    qown[...] = qsum[pl.ds(pl.multiple_of(core * 32, 32), 32), :]
    out[16 * NODE :] = qsum[pl.ds(pl.multiple_of((1 - core) * 32, 32), 32), :].astype(BF16)
    lhs = back_all(bt)

    @pl.loop(0, 16)
    def _(i):
        row = pl.multiple_of(i * NODE, NODE)
        g = backward_block(dense, lhs, z, x, 1 - core, i % 4, i // 4)
        out[pl.ds(row, NODE), :] = g.astype(BF16)


def backward_own(pos, dense, bt, got, qown, x0, z0, x1, x2, x3, z1, z2, z3, qs):
    z, x, core = pos[PZ], pos[PX], pos[PC]
    qs[...] = qown[...] + got[16 * NODE :].astype(F32)
    lhs = back_all(bt)
    xs, zs = (x0, x1, x2, x3), (z0, z1, z2, z3)
    for dx in range(4):
        for dz in range(4):
            i = (dx * 4 + dz) * NODE
            g = backward_block(dense, lhs, z, x, core, dz, dx) + got[i : i + NODE].astype(F32)
            xs[dx][dz * HALF : (dz + 1) * HALF] = g[:HALF].astype(xs[dx].dtype)
            zs[dz][dx * HALF : (dx + 1) * HALF] = g[HALF:].astype(zs[dz].dtype)


def first_sum(x0, x1, x2, x3, z0, z1, z2, z3, t0, a1, a2, a3, t1, b1, b2, b3):
    for parts, outs in (((x0, x1, x2, x3), (t0, a1, a2, a3)), ((z0, z1, z2, z3), (t1, b1, b2, b3))):
        for d in range(4):
            at = slice(d * HALF, (d + 1) * HALF)
            s = parts[0][at]
            for p in parts[1:]:
                s += p[at].astype(F32)
            outs[d][...] = s.astype(outs[d].dtype)


def last_sum(t0, a1, a2, a3, t1, b1, b2, b3, out):
    h0, h1 = t0[...], t1[...]
    for p in (a1, a2, a3):
        h0 += p[...].astype(F32)
    for p in (b1, b2, b3):
        h1 += p[...].astype(F32)
    out[...] = jnp.concatenate([h0, h1], axis=0).T.astype(BF16)


def ring_sum(axis, pos, own, r1, r2, r3, out, held):
    i = pos[axis]
    for d, r in enumerate((own, r1, r2, r3)):
        held[lax.rem(i + 4 - d, 4)] = r[...]
    out[...] = (held[0] + held[1]) + (held[2] + held[3])


def weight_rows(pos, own, r1, r2, r3, out):
    y = pos[PY]
    for d, r in enumerate((own, r1, r2, r3)):
        row = pl.multiple_of(lax.rem(y + 4 - d, 4) * 64, 64)
        out[pl.ds(row, 64), :] = r[...] * (1.0 / NODE)


def weight_pair(pos, own, other, out):
    core = pos[PC]
    out[pl.ds(pl.multiple_of(core * 32, 32), 32), :] = own[...]
    out[pl.ds(pl.multiple_of((1 - core) * 32, 32), 32), :] = other[...]


def send(v, axis, d, n=4):
    return lax.ppermute(v, axis, [(i, (i + d) % n) for i in range(n)])


def body(features, cotangent, weight, tile_values, tile_rows, tile_cols, tile_count):
    tv, rows, cols, count = tile_values[0, 0], tile_rows[0, 0], tile_cols[0, 0], tile_count[0]
    pos = jnp.stack([lax.axis_index(a) for a in ("z", "x", "core", "y")]).astype(jnp.int32)
    big = NCT * ROWS * TILE

    px = [send(features, "x", -d) for d in (1, 2, 3)]
    pz = [send(features, "z", -d) for d in (1, 2, 3)]
    part = 128
    dense_out = pltpu.VMEM((NCT, ROWS, TILE), BF16)
    dense = call(
        functools.partial(dense_first, part),
        dense_out,
        [ASPEC, SSPEC, SSPEC, SSPEC],
        [pltpu.SemaphoreType.DMA],
        nbytes=12 * MIB,
    )(tv, rows, cols, count)
    fx = jnp.concatenate([p[:HALF] for p in px], axis=0)
    fz = jnp.concatenate([p[HALF:] for p in pz], axis=0)
    zf = [send(fx, "z", -d) for d in (1, 2, 3)]
    xf = [send(fz, "x", -d) for d in (1, 2, 3)]
    near = jnp.concatenate([features] + px + pz, axis=0)
    near_other = send(near, "core", 1, 2)
    dense = call(
        functools.partial(dense_rest, part),
        dense_out,
        [ASPEC, SSPEC, SSPEC, SSPEC, VSPEC],
        [pltpu.SemaphoreType.DMA],
        nbytes=24 * MIB,
        aliases={4: 0},
    )(tv, rows, cols, count, in_vmem(dense))
    dense = in_vmem(dense)
    far = jnp.concatenate(zf + xf, axis=0)
    far_other = send(far, "core", 1, 2)

    acc = call(
        forward_own,
        shape((ROWS, FEAT), F32),
        [SSPEC, VSPEC, VSPEC, VSPEC],
        flops=big * FEAT,
        nbytes=big,
    )(pos, dense, near, far)
    block = shape((NODE, FEAT), BF16)
    own, s1, s2, s3 = call(
        forward_other,
        [shape((NODE, FEAT), F32), block, block, block],
        [SSPEC] + [VSPEC] * 4,
        [pltpu.VMEM((ROWS, FEAT), F32)],
        flops=big * FEAT,
        nbytes=big,
    )(pos, dense, near_other, far_other, acc)
    r = [send(s, "y", d) for d, s in ((1, s1), (2, s2), (3, s3))]

    packed = shape((NODE + 64, FEAT), BF16)
    activated, bt, q, m1, m2, m3 = call(
        middle,
        [block, block, shape((64, FEAT), F32), packed, packed, packed],
        [SSPEC] + [VSPEC] * 6,
        [pltpu.VMEM((FEAT, FEAT), F32)],
        flops=6 * FEAT**3,
        nbytes=MIB,
    )(pos, own, *r, weight, cotangent)
    r = [send(m, "y", d) for d, m in ((1, m1), (2, m2), (3, m3))]

    other, bt, qown = call(
        backward_other,
        [shape((16 * NODE + 32, FEAT), BF16), shape((4, FEAT, NODE), BF16), shape((32, FEAT), F32)],
        [SSPEC] + [VSPEC] * 6,
        [pltpu.VMEM((64, FEAT), F32)],
        flops=big * FEAT,
        nbytes=big,
    )(pos, dense, bt, *r, q)
    got = send(other, "core", 1, 2)
    long, longf = shape((4 * HALF, FEAT), BF16), shape((4 * HALF, FEAT), F32)
    x0, z0, x1, x2, x3, z1, z2, z3, qs = call(
        backward_own,
        [longf, longf] + [long] * 6 + [shape((32, FEAT), F32)],
        [SSPEC] + [VSPEC] * 4,
        flops=big * FEAT,
        nbytes=big,
    )(pos, dense, bt, got, qown)
    rx = [send(v, "x", d) for d, v in ((1, x1), (2, x2), (3, x3))]
    rz = [send(v, "z", d) for d, v in ((1, z1), (2, z2), (3, z3))]

    def ring(axis, place, v):
        got = [send(v, axis, d) for d in (1, 2, 3)]
        return call(
            functools.partial(ring_sum, place),
            shape(v.shape, F32),
            [SSPEC] + [VSPEC] * 4,
            [pltpu.VMEM((4,) + v.shape, F32)],
            nbytes=MIB // 4,
        )(pos, v, *got)

    qs = ring("z", PZ, ring("x", PX, qs))
    pair = call(weight_pair, shape((64, FEAT), F32), [SSPEC, VSPEC, VSPEC], nbytes=MIB // 8)(
        pos, qs, send(qs, "core", 1, 2)
    )
    weight_grad = call(
        weight_rows, shape((FEAT, FEAT), F32), [SSPEC] + [VSPEC] * 4, nbytes=MIB // 2
    )(pos, pair, *[send(pair, "y", d) for d in (1, 2, 3)])

    short, shortf = shape((HALF, FEAT), BF16), shape((HALF, FEAT), F32)
    t0, a1, a2, a3, t1, b1, b2, b3 = call(
        first_sum,
        [shortf, short, short, short] * 2,
        [VSPEC] * 8,
        nbytes=4 * MIB,
    )(x0, *rx, z0, *rz)
    ra = [send(v, "z", d) for d, v in ((1, a1), (2, a2), (3, a3))]
    rb = [send(v, "x", d) for d, v in ((1, b1), (2, b2), (3, b3))]
    feature_grad = call(last_sum, block, [VSPEC] * 8, nbytes=MIB)(t0, *ra, t1, *rb)
    return activated, weight_grad, feature_grad


def solution(mesh):
    parts = Mesh(mesh.devices.reshape(4, 4, 2, 4), ("z", "x", "core", "y"))
    row = ("z", "x", "core")
    return jax.shard_map(
        body,
        mesh=parts,
        in_specs=(
            P(("y",) + row, None),
            P(row + ("y",), None),
            P(),
            P(row, "y", None, None, None),
            P(row, "y", None),
            P(row, "y", None),
            P(row, "y"),
        ),
        out_specs=(P(row + ("y",), None), P(), P(("y",) + row, None)),
        check_vma=False,
    )
```

```python
import functools

import jax
import jax.numpy as jnp
from jax import lax
from jax.experimental import pallas as pl
from jax.experimental.pallas import tpu as pltpu
from jax.sharding import Mesh
from jax.sharding import PartitionSpec as P

F32 = jnp.float32
BF16 = jnp.bfloat16
TILE = 128
FEAT = 256
NODE = 256
HALF = 128
ROWS = 1024
NCT = 64
CAP = 384
MIB = 1 << 20
PZ, PX, PC, P1, P2, PY, PY1, PY2, PY3 = range(9)
RING = ("z", "x", "core")


def shape(s, dt):
    return jax.ShapeDtypeStruct(s, dt)


VSPEC = pl.BlockSpec(memory_space=pltpu.VMEM)
SSPEC = pl.BlockSpec(memory_space=pltpu.SMEM)
ASPEC = pl.BlockSpec(memory_space=pl.ANY)


def in_vmem(x):
    return pltpu.with_memory_space_constraint(x, pltpu.VMEM)


def call(kernel, outs, in_specs, scratch=(), flops=0, nbytes=0, limit=16, aliases=None):
    return pl.pallas_call(
        kernel,
        out_shape=outs,
        in_specs=in_specs,
        out_specs=jax.tree.map(lambda _: VSPEC, outs),
        scratch_shapes=list(scratch),
        input_output_aliases=aliases or {},
        cost_estimate=pl.CostEstimate(flops=flops, bytes_accessed=nbytes, transcendentals=0),
        compiler_params=pltpu.CompilerParams(vmem_limit_bytes=limit * MIB),
    )


DENSE = pltpu.VMEM((NCT, ROWS, TILE), BF16)
SIZE = NCT * ROWS * TILE


def dense_call(kernel, outs, dense, pos, *rest, scratch=(), cost=1000):
    n = 2 + len(rest)

    def wrapped(*refs):
        kernel(*refs[:n], *refs[n + 1 :])

    return call(
        wrapped,
        [DENSE] + outs,
        [SSPEC] + [VSPEC] * (n - 1),
        scratch,
        flops=cost,
        nbytes=cost,
        aliases={1: 0},
    )(pos, in_vmem(dense), *rest)


def dense_block(tv, rows, cols, count, dense, done, sem):
    def copy(s):
        return pltpu.make_async_copy(
            tv.at[s],
            dense.at[cols[s], pl.ds(pl.multiple_of(rows[s] * TILE, TILE), TILE), :],
            sem,
        )

    def start(s, _):
        copy(s).start()
        return 0

    def wait(s, _):
        copy(s).wait()
        return 0

    @pl.loop(0, NCT)
    def _(c):
        dense[c] = jnp.zeros((ROWS, TILE), BF16)

    lax.fori_loop(0, count[0], start, 0)
    lax.fori_loop(0, count[0], wait, 0)
    done[...] = jnp.zeros_like(done)


def column_tile(pos, core, e, d):
    z = lax.rem(pos[PZ] + d + core * (e - d), 4)
    x = lax.rem(pos[PX] + e + core * (d - e), 4)
    return 2 * (z * 8 + x * 2 + core)


def forward_own(pos, dense, near, far, done, acc):
    del done
    for d in range(4):
        lhs = []
        for e in range(4):
            c = column_tile(pos, pos[PC], e, d)
            lhs += [dense[c], dense[c + 1]]
        rhs = near[...] if d == 0 else far[(d - 1) * ROWS : d * ROWS]
        term = jnp.dot(jnp.concatenate(lhs, axis=1), rhs, preferred_element_type=F32)
        if d == 0:
            acc[...] = term
        else:
            acc[...] += term


def forward_other(blocks, pos, dense, near, far, given, *outs):
    rows = [pl.ds(pl.multiple_of(pos[b] * NODE, NODE), NODE) for b in blocks]
    total = jnp.concatenate([given[r, :] for r in rows], axis=0)
    for d in range(4):
        lhs = []
        for e in range(4):
            c = column_tile(pos, 1 - pos[PC], e, d)
            lhs += [jnp.concatenate([dense[c + i, r, :] for r in rows], axis=0) for i in range(2)]
        rhs = near[...] if d == 0 else far[(d - 1) * ROWS : d * ROWS]
        total += jnp.dot(jnp.concatenate(lhs, axis=1), rhs, preferred_element_type=F32)
    n = total.shape[0] // len(outs)
    for i, out in enumerate(outs):
        out[...] = total[i * n : (i + 1) * n].astype(out.dtype)


def middle(pos, own, r1, r2, r3, w, cot, act, bt, q, m1, m2, m3, lg):
    agg = (own[...] + r1[...].astype(F32) + r2[...].astype(F32) + r3[...].astype(F32)).astype(BF16)
    pre = jnp.dot(agg, w[...], preferred_element_type=F32)
    sg = jax.nn.sigmoid(pre)
    act[...] = (pre * sg).astype(BF16)
    dz = (cot[...].astype(F32) * sg * (1.0 + pre * (1.0 - sg))).astype(BF16)
    back = lax.dot_general(w[...], dz, (((1,), (1,)), ((), ())), preferred_element_type=F32).astype(
        BF16
    )
    lg[...] = lax.dot_general(agg, dz, (((0,), (0,)), ((), ())), preferred_element_type=F32)
    bt[...] = back
    for p, out in ((PY, q), (PY1, m1), (PY2, m2), (PY3, m3)):
        piece = lg[pl.ds(pl.multiple_of(pos[p] * 64, 64), 64), :]
        if p == PY:
            out[...] = piece
        else:
            out[:NODE] = back
            out[NODE:] = piece.astype(BF16)


FIRST, LAST = (2, 1), (3, 0)


def back_all(bt):
    return jnp.concatenate([bt[0], bt[1], bt[2], bt[3]], axis=1)


def backward_block(dense, lhs, pos, core, e, d):
    c = column_tile(pos, core, e, d)
    rhs = jnp.concatenate([dense[c], dense[c + 1]], axis=1)
    return jnp.dot(lhs, rhs, preferred_element_type=F32)


def two_parts(v):
    hi = v.astype(BF16)
    return hi, (v - hi.astype(F32)).astype(BF16)


def backward_other(distances, dense, lhs, pos, out):
    for k, e in enumerate(distances):
        for d in range(4):
            i = (k * 4 + d) * NODE
            out[i : i + NODE] = backward_block(dense, lhs, pos, 1 - pos[PC], e, d).astype(BF16)


def backward_other_first(pos, dense, own, r1, r2, r3, q, out, bt, qown, qsum):
    core, y = pos[PC], pos[PY]
    bt[y] = own[...]
    total = q[...]
    for d, r in ((1, r1), (2, r2), (3, r3)):
        bt[lax.rem(y + 4 - d, 4)] = r[:NODE]
        total += r[NODE:].astype(F32)
    qsum[...] = total
    qown[...] = qsum[pl.ds(pl.multiple_of(core * 32, 32), 32), :]
    out[8 * NODE :] = qsum[pl.ds(pl.multiple_of((1 - core) * 32, 32), 32), :].astype(BF16)
    backward_other(FIRST, dense, back_all(bt), pos, out)


def backward_other_last(pos, dense, bt, out):
    backward_other(LAST, dense, back_all(bt), pos, out)


def backward_own(distances, dense, lhs, pos, got, outs, hi, lo):
    for k, (e, out) in enumerate(zip(distances, outs, strict=True)):
        for d in range(4):
            i = (k * 4 + d) * NODE
            g = backward_block(dense, lhs, pos, pos[PC], e, d) + got[i : i + NODE].astype(F32)
            out[d * NODE : (d + 1) * NODE] = g.astype(out.dtype)
        if e:
            out[4 * NODE : 4 * NODE + 32] = hi
            out[4 * NODE + 32 :] = lo


def backward_own_first(pos, dense, bt, got, qown, x2, x1, qs):
    hi, lo = two_parts(qown[...] + got[8 * NODE :].astype(F32))
    qs[...] = hi.astype(F32) + lo.astype(F32)
    backward_own(FIRST, dense, back_all(bt), pos, got, (x2, x1), hi, lo)


def backward_own_last(pos, dense, bt, got, qs, x3, x0):
    hi, lo = two_parts(qs[...])
    backward_own(LAST, dense, back_all(bt), pos, got, (x3, x0), hi, lo)


def ring_sum(place, own, received, held):
    held[place] = own
    for d, (hi, lo) in received:
        held[lax.rem(place + 4 - d, 4)] = hi.astype(F32) + lo.astype(F32)
    return (held[0] + held[1]) + (held[2] + held[3])


def weight_parts(received, at):
    return [(d, (r[at : at + 32], r[at + 32 :])) for d, r in enumerate(received, 1)]


def first_sum(pos, x0, r1, r2, r3, qs, t0, t1, t2, t3, qt, held):
    hi, lo = two_parts(ring_sum(pos[P1], qs[...], weight_parts((r1, r2, r3), 4 * NODE), held))
    qt[...] = hi.astype(F32) + lo.astype(F32)
    for d, out in enumerate((t0, t1, t2, t3)):
        at = slice(d * NODE, (d + 1) * NODE)
        s = x0[at]
        for r in (r1, r2, r3):
            s += r[at].astype(F32)
        if d:
            out[:NODE] = s.astype(BF16)
            out[NODE : NODE + 32] = hi
            out[NODE + 32 :] = lo
        else:
            out[...] = s


def weight_sum(pos, r1, r2, r3, qt, qu, held):
    qu[...] = ring_sum(pos[P2], qt[...], weight_parts((r1, r2, r3), NODE), held)


def last_sum(t0, r1, r2, r3, out):
    s = t0[...]
    for r in (r1, r2, r3):
        s += r[:NODE].astype(F32)
    out[...] = s.T.astype(BF16)


def weight_rows(pos, own, r1, r2, r3, out):
    core = pos[PC]
    for p, r in ((PY, own), (PY3, r1), (PY2, r2), (PY1, r3)):
        for c, at in ((core, 0), (1 - core, 32)):
            row = pl.multiple_of(pos[p] * 64 + c * 32, 32)
            out[pl.ds(row, 32), :] = r[at : at + 32] * (1.0 / NODE)


def send(v, axis, d, n=4):
    return lax.ppermute(v, axis, [(i, (i + d) % n) for i in range(n)])


def send_by_core(v, stage, d):
    pairs = []
    for z in range(4):
        for x in range(4):
            for core in range(2):
                if core == stage:
                    to = z, (x + d) % 4
                else:
                    to = (z + d) % 4, x
                pairs.append((z * 8 + x * 2 + core, to[0] * 8 + to[1] * 2 + core))
    return lax.ppermute(v, RING, pairs)


def body(features, cotangent, weight, tile_values, tile_rows, tile_cols, tile_count):
    tv, rows, cols, count = tile_values[0, 0], tile_rows[0, 0], tile_cols[0, 0], tile_count[0]
    z, x, core, y = (lax.axis_index(a) for a in ("z", "x", "core", "y"))
    zero = core == 0
    places = [z, x, core, jnp.where(zero, x, z), jnp.where(zero, z, x)]
    places += [lax.rem(y + d, 4) for d in range(4)]
    pos = jnp.stack(places).astype(jnp.int32)
    tv = pltpu.with_memory_space_constraint(tv, pltpu.HBM)

    near = {d: send_by_core(features, 0, -d) for d in (2, 1, 3)}
    near = jnp.concatenate([features] + [near[d] for d in (1, 2, 3)], axis=0)
    near, count, pos = lax.optimization_barrier((near, count, pos))
    far = {d: send_by_core(near, 1, -d) for d in (2, 1, 3)}
    near_other = send(near, "core", 1, 2)
    dense, done = call(
        dense_block,
        [DENSE, shape((8, 128), F32)],
        [ASPEC, SSPEC, SSPEC, SSPEC],
        [pltpu.SemaphoreType.DMA],
        nbytes=24 * MIB,
    )(tv, rows, cols, count)
    far = jnp.concatenate([far[d] for d in (1, 2, 3)], axis=0)
    far, done = lax.optimization_barrier((far, done))
    far_other = send(far, "core", 1, 2)

    dense, acc = dense_call(forward_own, [shape((ROWS, FEAT), F32)], dense, pos, near, far, done)
    block, blockf = shape((NODE, FEAT), BF16), shape((NODE, FEAT), F32)

    def other_columns(dense, blocks, outs):
        kernel = functools.partial(forward_other, blocks)
        return dense_call(kernel, outs, dense, pos, near_other, far_other, acc)

    dense, s2, s1 = other_columns(dense, (PY2, PY1), [block, block])
    r2, r1 = send(s2, "y", 2), send(s1, "y", 1)
    dense, s3, own = other_columns(dense, (PY3, PY), [block, blockf])
    r3 = send(s3, "y", 3)

    packed = shape((NODE + 64, FEAT), BF16)
    activated, bt, q, m1, m2, m3 = call(
        middle,
        [block, block, shape((64, FEAT), F32), packed, packed, packed],
        [SSPEC] + [VSPEC] * 6,
        [pltpu.VMEM((FEAT, FEAT), F32)],
        flops=6 * FEAT**3,
        nbytes=MIB,
    )(pos, own, r1, r2, r3, weight, cotangent)
    r = {d: send(m, "y", d) for d, m in ((2, m2), (1, m1), (3, m3))}

    piece = shape((32, FEAT), F32)
    dense, other, bt, qown = dense_call(
        backward_other_first,
        [shape((8 * NODE + 32, FEAT), BF16), shape((4, FEAT, NODE), BF16), piece],
        dense, pos, bt, r[1], r[2], r[3], q,
        scratch=[pltpu.VMEM((64, FEAT), F32)],
    )
    got_first = send(other, "core", 1, 2)
    dense, other = dense_call(
        backward_other_last, [shape((8 * NODE, FEAT), BF16)], dense, pos, bt,
    )
    got_last = send(other, "core", 1, 2)
    long = shape((4 * NODE + 64, FEAT), BF16)
    dense, x2, x1, qs = dense_call(
        backward_own_first, [long, long, piece], dense, pos, bt, got_first, qown,
    )
    r = {2: send_by_core(x2, 0, 2), 1: send_by_core(x1, 0, 1)}
    dense, x3, x0 = dense_call(
        backward_own_last,
        [long, shape((4 * NODE, FEAT), F32)],
        dense, pos, bt, got_last, qs,
    )
    r[3] = send_by_core(x3, 0, 3)
    t0, t1, t2, t3, qt = call(
        first_sum,
        [blockf, packed, packed, packed, piece],
        [SSPEC] + [VSPEC] * 5,
        [pltpu.VMEM((4, 32, FEAT), F32)],
        nbytes=4 * MIB,
    )(pos, x0, r[1], r[2], r[3], qs)
    r = {d: send_by_core(v, 1, d) for d, v in ((2, t2), (1, t1), (3, t3))}
    qu = call(
        weight_sum,
        piece,
        [SSPEC] + [VSPEC] * 4,
        [pltpu.VMEM((4, 32, FEAT), F32)],
        nbytes=MIB // 4,
    )(pos, r[1], r[2], r[3], qt)
    pair = jnp.concatenate([qu, send(qu, "core", 1, 2)], axis=0)
    feature_grad = call(last_sum, block, [VSPEC] * 4, nbytes=MIB)(t0, r[1], r[2], r[3])
    r = {d: send(pair, "y", d) for d in (2, 1, 3)}
    weight_grad = call(
        weight_rows, shape((FEAT, FEAT), F32), [SSPEC] + [VSPEC] * 4, nbytes=MIB // 2
    )(pos, pair, r[1], r[2], r[3])
    return activated, weight_grad, feature_grad


def solution(mesh):
    parts = Mesh(mesh.devices.reshape(4, 4, 2, 4), ("z", "x", "core", "y"))
    return jax.shard_map(
        body,
        mesh=parts,
        in_specs=(
            P(("y",) + RING, None),
            P(RING + ("y",), None),
            P(),
            P(RING, "y", None, None, None),
            P(RING, "y", None),
            P(RING, "y", None),
            P(RING, "y"),
        ),
        out_specs=(P(RING + ("y",), None), P(), P(("y",) + RING, None)),
        check_vma=False,
    )
```

```python
import functools

import jax
import jax.numpy as jnp
from jax import lax
from jax.experimental import pallas as pl
from jax.experimental.pallas import tpu as pltpu
from jax.sharding import Mesh
from jax.sharding import PartitionSpec as P

F32 = jnp.float32
BF16 = jnp.bfloat16
TILE = 128
FEAT = 256
NODE = 256
HALF = 128
ROWS = 1024
NCT = 64
CAP = 384
MIB = 1 << 20
PZ, PX, PC, P1, P2, PY, PY1, PY2, PY3, PX1, PX3 = range(11)
RING = ("z", "x", "core")


def shape(s, dt):
    return jax.ShapeDtypeStruct(s, dt)


VSPEC = pl.BlockSpec(memory_space=pltpu.VMEM)
SSPEC = pl.BlockSpec(memory_space=pltpu.SMEM)
ASPEC = pl.BlockSpec(memory_space=pl.ANY)


def in_vmem(x):
    return pltpu.with_memory_space_constraint(x, pltpu.VMEM)


def call(kernel, outs, in_specs, scratch=(), flops=0, nbytes=0, limit=16, aliases=None):
    return pl.pallas_call(
        kernel,
        out_shape=outs,
        in_specs=in_specs,
        out_specs=jax.tree.map(lambda _: VSPEC, outs),
        scratch_shapes=list(scratch),
        input_output_aliases=aliases or {},
        cost_estimate=pl.CostEstimate(flops=flops, bytes_accessed=nbytes, transcendentals=0),
        compiler_params=pltpu.CompilerParams(vmem_limit_bytes=limit * MIB),
    )


DENSE = pltpu.VMEM((NCT, ROWS, TILE), BF16)
SIZE = NCT * ROWS * TILE


def dense_call(kernel, outs, dense, pos, *rest, scratch=(), cost=1000):
    n = 2 + len(rest)

    def wrapped(*refs):
        kernel(*refs[:n], *refs[n + 1 :])

    return call(
        wrapped,
        [DENSE] + outs,
        [SSPEC] + [VSPEC] * (n - 1),
        scratch,
        flops=cost,
        nbytes=cost,
        aliases={1: 0},
    )(pos, in_vmem(dense), *rest)


def dense_block(tv, rows, cols, count, dense, sem):
    def copy(s):
        return pltpu.make_async_copy(
            tv.at[s],
            dense.at[cols[s], pl.ds(pl.multiple_of(rows[s] * TILE, TILE), TILE), :],
            sem,
        )

    def start(s, _):
        copy(s).start()
        return 0

    def wait(s, _):
        copy(s).wait()
        return 0

    @pl.loop(0, NCT)
    def _(c):
        dense[c] = jnp.zeros((ROWS, TILE), BF16)

    lax.fori_loop(0, count[0], start, 0)
    lax.fori_loop(0, count[0], wait, 0)


def column_tile(pos, core, e, d):
    z = lax.rem(pos[PZ] + d + core * (e - d), 4)
    x = lax.rem(pos[PX] + e + core * (d - e), 4)
    return 2 * (z * 8 + x * 2 + core)


def tiles_of(dense, pos, core, d, rows):
    tiles = []
    for e in range(4):
        c = column_tile(pos, core, e, d)
        tiles += [jnp.concatenate([dense[c + i, r, :] for r in rows], axis=0) for i in range(2)]
    return jnp.concatenate(tiles, axis=1)


WHOLE = (slice(None),)


def forward_near(pos, dense, near, near_other, acc):
    core = pos[PC]
    acc[...] = jnp.dot(
        tiles_of(dense, pos, core, 0, WHOLE), near[...], preferred_element_type=F32
    ) + jnp.dot(
        tiles_of(dense, pos, 1 - core, 0, WHOLE), near_other[...], preferred_element_type=F32
    )


def far_sum(total, dense, pos, core, far, rows):
    for d in range(1, 4):
        rhs = far[(d - 1) * ROWS : d * ROWS]
        total += jnp.dot(tiles_of(dense, pos, core, d, rows), rhs, preferred_element_type=F32)
    return total


def forward_own(pos, dense, far, given, acc):
    acc[...] = far_sum(given[...], dense, pos, pos[PC], far, WHOLE)


def forward_other(blocks, pos, dense, far, given, *outs):
    rows = [pl.ds(pl.multiple_of(pos[b] * NODE, NODE), NODE) for b in blocks]
    total = jnp.concatenate([given[r, :] for r in rows], axis=0)
    total = far_sum(total, dense, pos, 1 - pos[PC], far, rows)
    for i, out in enumerate(outs):
        out[...] = total[i * NODE : (i + 1) * NODE].astype(out.dtype)


def add_two(own, r1, r2, out):
    out[...] = own[...] + r1[...].astype(F32) + r2[...].astype(F32)


def middle(pos, own, r3, w, cot, act, bt, q, m1, m2, m3, lg):
    agg = (own[...] + r3[...].astype(F32)).astype(BF16)
    pre = jnp.dot(agg, w[...], preferred_element_type=F32)
    sg = jax.nn.sigmoid(pre)
    act[...] = (pre * sg).astype(BF16)
    dz = (cot[...].astype(F32) * sg * (1.0 + pre * (1.0 - sg))).astype(BF16)
    back = lax.dot_general(w[...], dz, (((1,), (1,)), ((), ())), preferred_element_type=F32).astype(
        BF16
    )
    lg[...] = lax.dot_general(agg, dz, (((0,), (0,)), ((), ())), preferred_element_type=F32)
    bt[...] = back
    for p, out in ((PY, q), (PY1, m1), (PY2, m2), (PY3, m3)):
        piece = lg[pl.ds(pl.multiple_of(pos[p] * 64, 64), 64), :]
        if p == PY:
            out[...] = piece
        else:
            out[:NODE] = back
            out[NODE:] = piece.astype(BF16)


FIRST, LAST = (1, 3), (2, 0)


def back_all(bt):
    return jnp.concatenate([bt[0], bt[1], bt[2], bt[3]], axis=1)


def backward_block(dense, lhs, pos, core, e, d):
    c = column_tile(pos, core, e, d)
    rhs = jnp.concatenate([dense[c], dense[c + 1]], axis=1)
    return jnp.dot(lhs, rhs, preferred_element_type=F32)


def two_parts(v):
    hi = v.astype(BF16)
    return hi, (v - hi.astype(F32)).astype(BF16)


def backward_other(distances, dense, lhs, pos, out):
    for k, e in enumerate(distances):
        for d in range(4):
            i = (k * 4 + d) * NODE
            out[i : i + NODE] = backward_block(dense, lhs, pos, 1 - pos[PC], e, d).astype(BF16)


def backward_other_first(pos, dense, own, r1, r2, r3, q, out, bt, qown, qsum):
    core, y = pos[PC], pos[PY]
    bt[y] = own[...]
    total = q[...]
    for d, r in ((1, r1), (2, r2), (3, r3)):
        bt[lax.rem(y + 4 - d, 4)] = r[:NODE]
        total += r[NODE:].astype(F32)
    qsum[...] = total
    qown[...] = qsum[pl.ds(pl.multiple_of(core * 32, 32), 32), :]
    out[8 * NODE :] = qsum[pl.ds(pl.multiple_of((1 - core) * 32, 32), 32), :].astype(BF16)
    backward_other(FIRST, dense, back_all(bt), pos, out)


def backward_other_last(pos, dense, bt, out):
    backward_other(LAST, dense, back_all(bt), pos, out)


def backward_own(distances, dense, lhs, pos, got, outs, hi, lo):
    for k, (e, out) in enumerate(zip(distances, outs, strict=True)):
        for d in range(4):
            i = (k * 4 + d) * NODE
            g = backward_block(dense, lhs, pos, pos[PC], e, d) + got[i : i + NODE].astype(F32)
            out[d * NODE : (d + 1) * NODE] = g.astype(out.dtype)
        if e:
            out[4 * NODE : 4 * NODE + 32] = hi
            out[4 * NODE + 32 :] = lo


def backward_own_first(pos, dense, bt, got, qown, x1, x3, qs):
    hi, lo = two_parts(qown[...] + got[8 * NODE :].astype(F32))
    qs[...] = hi.astype(F32) + lo.astype(F32)
    backward_own(FIRST, dense, back_all(bt), pos, got, (x1, x3), hi, lo)


def backward_own_last(pos, dense, bt, got, qs, x2, x0):
    hi, lo = two_parts(qs[...])
    backward_own(LAST, dense, back_all(bt), pos, got, (x2, x0), hi, lo)


def ring_sum(place, own, received, held):
    held[place] = own
    for d, (hi, lo) in received:
        held[lax.rem(place + 4 - d, 4)] = hi.astype(F32) + lo.astype(F32)
    return (held[0] + held[1]) + (held[2] + held[3])


def weight_parts(received, at):
    return [(d, (r[at : at + 32], r[at + 32 :])) for d, r in enumerate(received, 1)]


def add_pair(own, r1, r3, out):
    n = 4 * NODE
    out[...] = own[...] + r1[:n].astype(F32) + r3[:n].astype(F32)


def first_sum(pos, x0, r1, r2, r3, qs, t0, t1, t2, t3, qt, held):
    hi, lo = two_parts(ring_sum(pos[P1], qs[...], weight_parts((r1, r2, r3), 4 * NODE), held))
    qt[...] = hi.astype(F32) + lo.astype(F32)
    for d, out in enumerate((t0, t1, t2, t3)):
        at = slice(d * NODE, (d + 1) * NODE)
        out[:NODE] = (x0[at] + r2[at].astype(F32)).astype(out.dtype)
        if d:
            out[NODE : NODE + 32] = hi
            out[NODE + 32 :] = lo


def weight_sum(pos, r1, r2, r3, qt, qu, held):
    qu[...] = ring_sum(pos[P2], qt[...], weight_parts((r1, r2, r3), NODE), held)


def last_sum(t0, r1, r2, r3, out):
    s = t0[...]
    for r in (r1, r2, r3):
        s += r[:NODE].astype(F32)
    out[...] = s.T.astype(BF16)


def weight_rows(pos, own, r1, r2, r3, out):
    core = pos[PC]
    for p, r in ((PY, own), (PY3, r1), (PY2, r2), (PY1, r3)):
        for c, at in ((core, 0), (1 - core, 32)):
            row = pl.multiple_of(pos[p] * 64 + c * 32, 32)
            out[pl.ds(row, 32), :] = r[at : at + 32] * (1.0 / NODE)


def send(v, axis, d, n=4):
    return lax.ppermute(v, axis, [(i, (i + d) % n) for i in range(n)])


def send_by_core(v, stage, d):
    pairs = []
    for z in range(4):
        for x in range(4):
            for core in range(2):
                if core == stage:
                    to = z, (x + d) % 4
                else:
                    to = (z + d) % 4, x
                pairs.append((z * 8 + x * 2 + core, to[0] * 8 + to[1] * 2 + core))
    return lax.ppermute(v, RING, pairs)


def body(features, cotangent, weight, tile_values, tile_rows, tile_cols, tile_count):
    tv, rows, cols, count = tile_values[0, 0], tile_rows[0, 0], tile_cols[0, 0], tile_count[0]
    z, x, core, y = (lax.axis_index(a) for a in ("z", "x", "core", "y"))
    zero = core == 0
    places = [z, x, core, jnp.where(zero, x, z), jnp.where(zero, z, x)]
    places += [lax.rem(y + d, 4) for d in range(4)] + [y ^ 1, y ^ 3]
    pos = jnp.stack(places).astype(jnp.int32)
    tv = pltpu.with_memory_space_constraint(tv, pltpu.HBM)

    near = {d: send_by_core(features, 0, -d) for d in (2, 1, 3)}
    near = jnp.concatenate([features] + [near[d] for d in (1, 2, 3)], axis=0)
    near, count, pos = lax.optimization_barrier((near, count, pos))
    far = {d: send_by_core(near, 1, -d) for d in (2, 1, 3)}
    near_other = send(near, "core", 1, 2)
    dense = call(
        dense_block,
        DENSE,
        [ASPEC, SSPEC, SSPEC, SSPEC],
        [pltpu.SemaphoreType.DMA],
        nbytes=24 * MIB,
    )(tv, rows, cols, count)
    sums = shape((ROWS, FEAT), F32)
    dense, acc = dense_call(forward_near, [sums], dense, pos, near, near_other, cost=16 * MIB)
    far, acc = lax.optimization_barrier((far, acc))
    far = jnp.concatenate([far[d] for d in (1, 2, 3)], axis=0)
    far_other = send(far, "core", 1, 2)
    dense, acc = dense_call(forward_own, [sums], dense, pos, far, acc)
    block, blockf = shape((NODE, FEAT), BF16), shape((NODE, FEAT), F32)

    def other_columns(dense, blocks, outs):
        kernel = functools.partial(forward_other, blocks)
        return dense_call(kernel, outs, dense, pos, far_other, acc)

    dense, s2, s1 = other_columns(dense, (PY2, PY1), [block, block])
    r2, r1 = send(s2, "y", 2), send(s1, "y", 1)
    dense, s3, own = other_columns(dense, (PY3, PY), [block, blockf])
    own = call(add_two, blockf, [VSPEC] * 3, nbytes=MIB // 2)(own, r1, r2)
    r3 = send(s3, "y", 3)

    packed = shape((NODE + 64, FEAT), BF16)
    activated, bt, q, m1, m2, m3 = call(
        middle,
        [block, block, shape((64, FEAT), F32), packed, packed, packed],
        [SSPEC] + [VSPEC] * 4,
        [pltpu.VMEM((FEAT, FEAT), F32)],
        flops=6 * FEAT**3,
        nbytes=MIB,
    )(pos, own, r3, weight, cotangent)
    r = {d: send(m, "y", d) for d, m in ((2, m2), (1, m1), (3, m3))}

    piece = shape((32, FEAT), F32)
    dense, other, bt, qown = dense_call(
        backward_other_first,
        [shape((8 * NODE + 32, FEAT), BF16), shape((4, FEAT, NODE), BF16), piece],
        dense, pos, bt, r[1], r[2], r[3], q,
        scratch=[pltpu.VMEM((64, FEAT), F32)],
    )
    got_first = send(other, "core", 1, 2)
    dense, other = dense_call(
        backward_other_last, [shape((8 * NODE, FEAT), BF16)], dense, pos, bt
    )
    got_last = send(other, "core", 1, 2)
    long, longf = shape((4 * NODE + 64, FEAT), BF16), shape((4 * NODE, FEAT), F32)
    dense, x1, x3, qs = dense_call(
        backward_own_first, [long, long, piece], dense, pos, bt, got_first, qown
    )
    r1, r3 = send_by_core(x1, 0, 1), send_by_core(x3, 0, 3)
    dense, x2, x0 = dense_call(backward_own_last, [long, longf], dense, pos, bt, got_last, qs)
    r2 = send_by_core(x2, 0, 2)
    held = [pltpu.VMEM((4, 32, FEAT), F32)]
    x0 = call(add_pair, longf, [VSPEC] * 3, nbytes=MIB)(x0, r1, r3)
    t0, t1, t2, t3, qt = call(
        first_sum,
        [blockf, packed, packed, packed, piece],
        [SSPEC] + [VSPEC] * 5,
        held,
        nbytes=MIB,
    )(pos, x0, r1, r2, r3, qs)
    r1, r2, r3 = (send_by_core(v, 1, d) for d, v in ((1, t1), (2, t2), (3, t3)))
    qu = call(weight_sum, piece, [SSPEC] + [VSPEC] * 4, held, nbytes=MIB // 4)(pos, r1, r2, r3, qt)
    pair = jnp.concatenate([qu, send(qu, "core", 1, 2)], axis=0)
    feature_grad = call(last_sum, block, [VSPEC] * 4, nbytes=MIB)(t0, r1, r2, r3)
    r = {d: send(pair, "y", d) for d in (2, 1, 3)}
    weight_grad = call(
        weight_rows, shape((FEAT, FEAT), F32), [SSPEC] + [VSPEC] * 4, nbytes=MIB // 2
    )(pos, pair, r[1], r[2], r[3])
    return activated, weight_grad, feature_grad


def solution(mesh):
    parts = Mesh(mesh.devices.reshape(4, 4, 2, 4), ("z", "x", "core", "y"))
    return jax.shard_map(
        body,
        mesh=parts,
        in_specs=(
            P(("y",) + RING, None),
            P(RING + ("y",), None),
            P(),
            P(RING, "y", None, None, None),
            P(RING, "y", None),
            P(RING, "y", None),
            P(RING, "y"),
        ),
        out_specs=(P(RING + ("y",), None), P(), P(("y",) + RING, None)),
        check_vma=False,
    )
```

```python
import functools

import jax
import jax.numpy as jnp
from jax import lax
from jax.experimental import pallas as pl
from jax.experimental.pallas import tpu as pltpu
from jax.sharding import Mesh
from jax.sharding import PartitionSpec as P

F32 = jnp.float32
BF16 = jnp.bfloat16
TILE = 128
FEAT = 256
NODE = 256
HALF = 128
ROWS = 1024
NCT = 64
CAP = 384
MIB = 1 << 20
PZ, PX, PC, PY, PY1, PY2, PY3, PX1, PX3 = range(9)
RING = ("z", "x", "core")


def shape(s, dt):
    return jax.ShapeDtypeStruct(s, dt)


VSPEC = pl.BlockSpec(memory_space=pltpu.VMEM)
SSPEC = pl.BlockSpec(memory_space=pltpu.SMEM)
ASPEC = pl.BlockSpec(memory_space=pl.ANY)


def in_vmem(x):
    return pltpu.with_memory_space_constraint(x, pltpu.VMEM)


def call(kernel, outs, in_specs, scratch=(), flops=0, nbytes=0, limit=16, aliases=None):
    return pl.pallas_call(
        kernel,
        out_shape=outs,
        in_specs=in_specs,
        out_specs=jax.tree.map(lambda _: VSPEC, outs),
        scratch_shapes=list(scratch),
        input_output_aliases=aliases or {},
        cost_estimate=pl.CostEstimate(flops=flops, bytes_accessed=nbytes, transcendentals=0),
        compiler_params=pltpu.CompilerParams(vmem_limit_bytes=limit * MIB),
    )


DENSE = pltpu.VMEM((NCT, ROWS, TILE), BF16)
SIZE = NCT * ROWS * TILE


def dense_call(kernel, outs, dense, pos, *rest, scratch=(), cost=1000):
    n = 2 + len(rest)

    def wrapped(*refs):
        kernel(*refs[:n], *refs[n + 1 :])

    return call(
        wrapped,
        [DENSE] + outs,
        [SSPEC] + [VSPEC] * (n - 1),
        scratch,
        flops=cost,
        nbytes=cost,
        aliases={1: 0},
    )(pos, in_vmem(dense), *rest)


def dense_block(tv, rows, cols, count, dense, sem):
    def copy(s):
        return pltpu.make_async_copy(
            tv.at[s],
            dense.at[cols[0, 0, s], pl.ds(pl.multiple_of(rows[0, 0, s] * TILE, TILE), TILE), :],
            sem,
        )

    def start(s, _):
        copy(s).start()
        return 0

    def wait(s, _):
        copy(s).wait()
        return 0

    @pl.loop(0, NCT)
    def _(c):
        dense[c] = jnp.zeros((ROWS, TILE), BF16)

    lax.fori_loop(0, count[0], start, 0)
    lax.fori_loop(0, count[0], wait, 0)


def column_tile(pos, core, e, d):
    z = lax.rem(pos[PZ] + d + core * (e - d), 4)
    x = lax.rem(pos[PX] + e + core * (d - e), 4)
    return 2 * (z * 8 + x * 2 + core)


def tiles_of(dense, pos, core, d, rows):
    tiles = []
    for e in range(4):
        c = column_tile(pos, core, e, d)
        tiles += [jnp.concatenate([dense[c + i, r, :] for r in rows], axis=0) for i in range(2)]
    return jnp.concatenate(tiles, axis=1)


WHOLE = (slice(None),)


def forward_near(pos, dense, near, near_other, acc):
    core = pos[PC]
    acc[...] = jnp.dot(
        tiles_of(dense, pos, core, 0, WHOLE), near[...], preferred_element_type=F32
    ) + jnp.dot(
        tiles_of(dense, pos, 1 - core, 0, WHOLE), near_other[...], preferred_element_type=F32
    )


def far_sum(total, dense, pos, core, far, rows):
    for d in range(1, 4):
        rhs = far[(d - 1) * ROWS : d * ROWS]
        total += jnp.dot(tiles_of(dense, pos, core, d, rows), rhs, preferred_element_type=F32)
    return total


def forward_own(pos, dense, far, given, acc):
    acc[...] = far_sum(given[...], dense, pos, pos[PC], far, WHOLE)


def forward_other(blocks, pos, dense, far, given, *outs):
    rows = [pl.ds(pl.multiple_of(pos[b] * NODE, NODE), NODE) for b in blocks]
    total = jnp.concatenate([given[r, :] for r in rows], axis=0)
    total = far_sum(total, dense, pos, 1 - pos[PC], far, rows)
    for i, out in enumerate(outs):
        out[...] = total[i * NODE : (i + 1) * NODE].astype(out.dtype)


def add_two(own, r1, r2, out):
    out[...] = own[...] + r1[...].astype(F32) + r2[...].astype(F32)


def middle(pos, own, r3, w, cot, act, bt, q, m1, m2, m3, lg):
    agg = (own[...] + r3[...].astype(F32)).astype(BF16)
    pre = jnp.dot(agg, w[...], preferred_element_type=F32)
    sg = jax.nn.sigmoid(pre)
    act[...] = (pre * sg).astype(BF16)
    dz = (cot[...].astype(F32) * sg * (1.0 + pre * (1.0 - sg))).astype(BF16)
    back = lax.dot_general(w[...], dz, (((1,), (1,)), ((), ())), preferred_element_type=F32).astype(
        BF16
    )
    lg[...] = lax.dot_general(agg, dz, (((0,), (0,)), ((), ())), preferred_element_type=F32)
    bt[...] = back
    for p, out in ((PY, q), (PY1, m1), (PY2, m2), (PY3, m3)):
        piece = lg[pl.ds(pl.multiple_of(pos[p] * 64, 64), 64), :]
        if p == PY:
            out[...] = piece
        else:
            out[:NODE] = back
            out[NODE:] = piece.astype(BF16)


FIRST, LAST = (1, 3), (2, 0)


def back_all(bt):
    return jnp.concatenate([bt[0], bt[1], bt[2], bt[3]], axis=1)


def backward_block(dense, lhs, pos, core, e, d):
    c = column_tile(pos, core, e, d)
    rhs = jnp.concatenate([dense[c], dense[c + 1]], axis=1)
    return jnp.dot(lhs, rhs, preferred_element_type=F32)


def backward_other(distances, dense, lhs, pos, out):
    for k, e in enumerate(distances):
        for d in range(4):
            i = (k * 4 + d) * NODE
            out[i : i + NODE] = backward_block(dense, lhs, pos, 1 - pos[PC], e, d).astype(BF16)


def two_parts(v):
    hi = v.astype(BF16)
    return hi, (v - hi.astype(F32)).astype(BF16)


def backward_other_first(pos, dense, own, r1, r2, r3, q, out, bt, qown):
    y = pos[PY]
    bt[y] = own[...]
    total = q[...]
    for d, r in ((1, r1), (2, r2), (3, r3)):
        bt[lax.rem(y + 4 - d, 4)] = r[:NODE]
        total += r[NODE:].astype(F32)
    hi, lo = two_parts(total)
    qown[...] = hi.astype(F32) + lo.astype(F32)
    out[8 * NODE : 8 * NODE + 64] = hi
    out[8 * NODE + 64 :] = lo
    backward_other(FIRST, dense, back_all(bt), pos, out)


def backward_other_last(pos, dense, bt, out):
    backward_other(LAST, dense, back_all(bt), pos, out)


def backward_own(distances, dense, bt, pos, got, outs):
    lhs = back_all(bt)
    for k, (e, out) in enumerate(zip(distances, outs, strict=True)):
        for d in range(4):
            i = (k * 4 + d) * NODE
            g = backward_block(dense, lhs, pos, pos[PC], e, d) + got[i : i + NODE].astype(F32)
            out[d * NODE : (d + 1) * NODE] = g.astype(out.dtype)


def ring_sum(place, terms, out, held):
    for d, term in enumerate(terms):
        held[lax.rem(place + 4 - d, 4)] = term[...]
    out[...] = (held[0] + held[1]) + (held[2] + held[3])


def backward_own_first(pos, dense, bt, got, qown, qsum, x1, x3):
    hi, lo = got[8 * NODE : 8 * NODE + 64], got[8 * NODE + 64 :]
    qsum[...] = qown[...] + (hi.astype(F32) + lo.astype(F32))
    backward_own(FIRST, dense, bt, pos, got, (x1, x3))


def backward_own_last(pos, dense, bt, got, q, q1, q2, q3, qsum, x2, x0, held):
    ring_sum(pos[PX], (q, q1, q2, q3), qsum, held)
    backward_own(LAST, dense, bt, pos, got, (x2, x0))


def first_sum(pos, x0, r2, q, q1, q2, q3, t0, t1, t2, t3, qsum, held):
    ring_sum(pos[PZ], (q, q1, q2, q3), qsum, held)
    for d, out in enumerate((t0, t1, t2, t3)):
        at = slice(d * NODE, (d + 1) * NODE)
        out[...] = (x0[at] + r2[at].astype(F32)).astype(out.dtype)


def last_sum(t0, r1, r2, r3, out):
    s = t0[...]
    for r in (r1, r2, r3):
        s += r[...].astype(F32)
    out[...] = s.T.astype(BF16)


def weight_rows(pos, first, second, out):
    for r, i, p in ((first, 0, PY), (first, 64, PX1), (second, 0, PX3), (second, 64, PY2)):
        row = pl.multiple_of(pos[p] * 64, 64)
        out[pl.ds(row, 64), :] = r[i : i + 64] * (1.0 / NODE)


def send(v, axis, d, n=4):
    return lax.ppermute(v, axis, [(i, (i + d) % n) for i in range(n)])


def swap(v, axis, step):
    return lax.ppermute(v, axis, [(i, i ^ step) for i in range(4)])


def send_by_core(v, stage, d):
    pairs = []
    for z in range(4):
        for x in range(4):
            for core in range(2):
                if core == stage:
                    to = z, (x + d) % 4
                else:
                    to = (z + d) % 4, x
                pairs.append((z * 8 + x * 2 + core, to[0] * 8 + to[1] * 2 + core))
    return lax.ppermute(v, RING, pairs)


def body(features, cotangent, weight, tile_values, tile_rows, tile_cols, tile_count):
    tv, rows, cols, count = tile_values[0, 0], tile_rows, tile_cols, tile_count[0]
    z, x, core, y = (lax.axis_index(a) for a in ("z", "x", "core", "y"))
    places = [z, x, core] + [lax.rem(y + d, 4) for d in range(4)] + [y ^ 1, y ^ 3]
    pos = jnp.stack(places).astype(jnp.int32)
    tv = pltpu.with_memory_space_constraint(tv, pltpu.HBM)

    near = {d: send_by_core(features, 0, -d) for d in (2, 1, 3)}
    near = jnp.concatenate([features] + [near[d] for d in (1, 2, 3)], axis=0)
    near, count, pos = lax.optimization_barrier((near, count, pos))
    far = {d: send_by_core(near, 1, -d) for d in (2, 1, 3)}
    near_other = send(near, "core", 1, 2)
    dense = call(
        dense_block,
        DENSE,
        [ASPEC, SSPEC, SSPEC, SSPEC],
        [pltpu.SemaphoreType.DMA],
        nbytes=24 * MIB,
    )(tv, rows, cols, count)
    sums = shape((ROWS, FEAT), F32)
    dense, acc = dense_call(forward_near, [sums], dense, pos, near, near_other, cost=16 * MIB)
    far, acc = lax.optimization_barrier((far, acc))
    far = jnp.concatenate([far[d] for d in (1, 2, 3)], axis=0)
    far_other = send(far, "core", 1, 2)
    dense, acc = dense_call(forward_own, [sums], dense, pos, far, acc)
    block, blockf = shape((NODE, FEAT), BF16), shape((NODE, FEAT), F32)

    def other_columns(dense, blocks, outs):
        kernel = functools.partial(forward_other, blocks)
        return dense_call(kernel, outs, dense, pos, far_other, acc)

    dense, s2, s1 = other_columns(dense, (PY2, PY1), [block, block])
    r2, r1 = send(s2, "y", 2), send(s1, "y", 1)
    dense, s3, own = other_columns(dense, (PY3, PY), [block, blockf])
    own = call(add_two, blockf, [VSPEC] * 3, nbytes=MIB // 2)(own, r1, r2)
    r3 = send(s3, "y", 3)

    packed = shape((NODE + 64, FEAT), BF16)
    activated, bt, q, m1, m2, m3 = call(
        middle,
        [block, block, shape((64, FEAT), F32), packed, packed, packed],
        [SSPEC] + [VSPEC] * 4,
        [pltpu.VMEM((FEAT, FEAT), F32)],
        flops=6 * FEAT**3,
        nbytes=MIB,
    )(pos, own, r3, weight, cotangent)
    r = {d: send(m, "y", d) for d, m in ((2, m2), (1, m1), (3, m3))}

    piece = shape((64, FEAT), F32)
    dense, other, bt, q = dense_call(
        backward_other_first,
        [shape((8 * NODE + 128, FEAT), BF16), shape((4, FEAT, NODE), BF16), piece],
        dense, pos, bt, r[1], r[2], r[3], q,
    )
    got_first = send(other, "core", 1, 2)
    dense, other = dense_call(
        backward_other_last, [shape((8 * NODE, FEAT), BF16)], dense, pos, bt
    )
    got_last = send(other, "core", 1, 2)
    long, longf = shape((4 * NODE, FEAT), BF16), shape((4 * NODE, FEAT), F32)

    held = [pltpu.VMEM((4, 64, FEAT), F32)]
    dense, q, x1, x3 = dense_call(
        backward_own_first, [piece, long, long], dense, pos, bt, got_first, q
    )
    along_x = [send(q, "x", d) for d in (1, 2, 3)]
    r1, r3 = send_by_core(x1, 0, 1), send_by_core(x3, 0, 3)
    dense, q, x2, x0 = dense_call(
        backward_own_last,
        [piece, long, longf],
        dense, pos, bt, got_last, q, *along_x,
        scratch=held,
    )
    r2 = send_by_core(x2, 0, 2)
    x0 = call(add_two, longf, [VSPEC] * 3, nbytes=MIB)(x0, r1, r3)
    t0, t1, t2, t3, q = call(
        first_sum,
        [blockf, block, block, block, piece],
        [SSPEC] + [VSPEC] * 6,
        held,
        nbytes=MIB,
    )(pos, x0, r2, q, *[send(q, "z", d) for d in (1, 2, 3)])
    r = {d: send_by_core(v, 1, d) for d, v in ((2, t2), (1, t1), (3, t3))}
    feature_grad = call(last_sum, block, [VSPEC] * 4, nbytes=MIB)(t0, r[1], r[2], r[3])
    first = jnp.concatenate([q, swap(q, "y", 1)], axis=0)
    weight_grad = call(
        weight_rows, shape((FEAT, FEAT), F32), [SSPEC, VSPEC, VSPEC], nbytes=MIB // 2
    )(pos, first, swap(first, "y", 3))
    return activated, weight_grad, feature_grad


def solution(mesh):
    parts = Mesh(mesh.devices.reshape(4, 4, 2, 4), ("z", "x", "core", "y"))
    return jax.shard_map(
        body,
        mesh=parts,
        in_specs=(
            P(("y",) + RING, None),
            P(RING + ("y",), None),
            P(),
            P(RING, "y", None, None, None),
            P(RING, "y", None),
            P(RING, "y", None),
            P(RING, "y"),
        ),
        out_specs=(P(RING + ("y",), None), P(), P(("y",) + RING, None)),
        check_vma=False,
    )
```

```python
import functools

import jax
import jax.numpy as jnp
from jax import lax
from jax.experimental import pallas as pl
from jax.experimental.pallas import tpu as pltpu
from jax.sharding import Mesh
from jax.sharding import PartitionSpec as P

F32 = jnp.float32
BF16 = jnp.bfloat16
TILE = 128
FEAT = 256
NODE = 256
HALF = 128
ROWS = 1024
NCT = 64
CAP = 384
MIB = 1 << 20
PZ, PX, PC, PY, PY1, PY2, PY3, PX1, PX3 = range(9)
RING = ("z", "x", "core")


def shape(s, dt):
    return jax.ShapeDtypeStruct(s, dt)


VSPEC = pl.BlockSpec(memory_space=pltpu.VMEM)
SSPEC = pl.BlockSpec(memory_space=pltpu.SMEM)
ASPEC = pl.BlockSpec(memory_space=pl.ANY)


def in_vmem(x):
    return pltpu.with_memory_space_constraint(x, pltpu.VMEM)


def call(kernel, outs, in_specs, scratch=(), flops=0, nbytes=0, limit=16, aliases=None):
    return pl.pallas_call(
        kernel,
        out_shape=outs,
        in_specs=in_specs,
        out_specs=jax.tree.map(lambda _: VSPEC, outs),
        scratch_shapes=list(scratch),
        input_output_aliases=aliases or {},
        cost_estimate=pl.CostEstimate(flops=flops, bytes_accessed=nbytes, transcendentals=0),
        compiler_params=pltpu.CompilerParams(vmem_limit_bytes=limit * MIB),
    )


DENSE = pltpu.VMEM((NCT, ROWS, TILE), BF16)
SIZE = NCT * ROWS * TILE


def dense_call(kernel, outs, dense, pos, *rest, scratch=(), cost=1000):
    n = 2 + len(rest)

    def wrapped(*refs):
        kernel(*refs[:n], *refs[n + 1 :])

    return call(
        wrapped,
        [DENSE] + outs,
        [SSPEC] + [VSPEC] * (n - 1),
        scratch,
        flops=cost,
        nbytes=cost,
        aliases={1: 0},
    )(pos, in_vmem(dense), *rest)


def dense_zeros(pos, dense):
    del pos

    @pl.loop(0, NCT)
    def _(c):
        dense[c] = jnp.zeros((ROWS, TILE), BF16)


def dense_block(tv, rows_in, cols_in, count, given, dense, rows, cols, sem, sem_rows, sem_cols):
    del given
    index_copies = (
        pltpu.make_async_copy(rows_in, rows, sem_rows),
        pltpu.make_async_copy(cols_in, cols, sem_cols),
    )
    for copy in index_copies:
        copy.start()
    for copy in index_copies:
        copy.wait()

    def tile(s):
        return pltpu.make_async_copy(
            tv.at[s],
            dense.at[cols[0, 0, s], pl.ds(pl.multiple_of(rows[0, 0, s] * TILE, TILE), TILE), :],
            sem,
        )

    def start(s, _):
        tile(s).start()
        return 0

    def wait(s, _):
        tile(s).wait()
        return 0

    lax.fori_loop(0, count[0], start, 0)
    lax.fori_loop(0, count[0], wait, 0)


def column_tile(pos, core, e, d):
    z = lax.rem(pos[PZ] + d + core * (e - d), 4)
    x = lax.rem(pos[PX] + e + core * (d - e), 4)
    return 2 * (z * 8 + x * 2 + core)


def tiles_of(dense, pos, core, d, rows):
    tiles = []
    for e in range(4):
        c = column_tile(pos, core, e, d)
        tiles += [jnp.concatenate([dense[c + i, r, :] for r in rows], axis=0) for i in range(2)]
    return jnp.concatenate(tiles, axis=1)


WHOLE = (slice(None),)


def forward_near(pos, dense, near, near_other, acc):
    core = pos[PC]
    acc[...] = jnp.dot(
        tiles_of(dense, pos, core, 0, WHOLE), near[...], preferred_element_type=F32
    ) + jnp.dot(
        tiles_of(dense, pos, 1 - core, 0, WHOLE), near_other[...], preferred_element_type=F32
    )


FAR = (1, 3, 2)


def far_sum(total, dense, pos, core, far, rows):
    for i, d in enumerate(FAR):
        rhs = far[i * ROWS : (i + 1) * ROWS]
        total += jnp.dot(tiles_of(dense, pos, core, d, rows), rhs, preferred_element_type=F32)
    return total


def forward_own(pos, dense, far, given, acc):
    acc[...] = far_sum(given[...], dense, pos, pos[PC], far, WHOLE)


def forward_other(blocks, pos, dense, far, given, *outs):
    rows = [pl.ds(pl.multiple_of(pos[b] * NODE, NODE), NODE) for b in blocks]
    total = jnp.concatenate([given[r, :] for r in rows], axis=0)
    total = far_sum(total, dense, pos, 1 - pos[PC], far, rows)
    for i, out in enumerate(outs):
        out[...] = total[i * NODE : (i + 1) * NODE].astype(out.dtype)


def add_two(own, r1, r2, out):
    out[...] = own[...] + r1[...].astype(F32) + r2[...].astype(F32)


def middle(pos, own, r3, w, cot, act, bt, q, m1, m2, m3, lg):
    agg = (own[...] + r3[...].astype(F32)).astype(BF16)
    pre = jnp.dot(agg, w[...], preferred_element_type=F32)
    sg = jax.nn.sigmoid(pre)
    act[...] = (pre * sg).astype(BF16)
    dz = (cot[...].astype(F32) * sg * (1.0 + pre * (1.0 - sg))).astype(BF16)
    back = lax.dot_general(w[...], dz, (((1,), (1,)), ((), ())), preferred_element_type=F32).astype(
        BF16
    )
    lg[...] = lax.dot_general(agg, dz, (((0,), (0,)), ((), ())), preferred_element_type=F32)
    bt[...] = back
    for p, out in ((PY, q), (PY1, m1), (PY2, m2), (PY3, m3)):
        piece = lg[pl.ds(pl.multiple_of(pos[p] * 64, 64), 64), :]
        if p == PY:
            out[...] = piece
        else:
            out[:NODE] = back
            out[NODE:] = piece.astype(BF16)


FIRST, LAST = (1, 3), (2, 0)


def back_all(bt):
    return jnp.concatenate([bt[0], bt[1], bt[2], bt[3]], axis=1)


def backward_block(dense, lhs, pos, core, e, d):
    c = column_tile(pos, core, e, d)
    rhs = jnp.concatenate([dense[c], dense[c + 1]], axis=1)
    return jnp.dot(lhs, rhs, preferred_element_type=F32)


def backward_other(distances, dense, lhs, pos, out):
    for k, e in enumerate(distances):
        for d in range(4):
            i = (k * 4 + d) * NODE
            out[i : i + NODE] = backward_block(dense, lhs, pos, 1 - pos[PC], e, d).astype(BF16)


def two_parts(v):
    hi = v.astype(BF16)
    return hi, (v - hi.astype(F32)).astype(BF16)


def backward_other_first(pos, dense, own, r1, r2, r3, q, out, bt, qown):
    y = pos[PY]
    bt[y] = own[...]
    total = q[...]
    for d, r in ((1, r1), (2, r2), (3, r3)):
        bt[lax.rem(y + 4 - d, 4)] = r[:NODE]
        total += r[NODE:].astype(F32)
    hi, lo = two_parts(total)
    qown[...] = hi.astype(F32) + lo.astype(F32)
    out[8 * NODE : 8 * NODE + 64] = hi
    out[8 * NODE + 64 :] = lo
    backward_other(FIRST, dense, back_all(bt), pos, out)


def backward_other_last(pos, dense, bt, out):
    backward_other(LAST, dense, back_all(bt), pos, out)


def backward_own(distances, dense, bt, pos, got, outs):
    lhs = back_all(bt)
    for k, (e, out) in enumerate(zip(distances, outs, strict=True)):
        for d in range(4):
            i = (k * 4 + d) * NODE
            g = backward_block(dense, lhs, pos, pos[PC], e, d) + got[i : i + NODE].astype(F32)
            out[d * NODE : (d + 1) * NODE] = g.astype(out.dtype)


def ring_sum(place, terms, out, held):
    for d, term in enumerate(terms):
        held[lax.rem(place + 4 - d, 4)] = term[...]
    out[...] = (held[0] + held[1]) + (held[2] + held[3])


def backward_own_first(pos, dense, bt, got, qown, qsum, x1, x3):
    hi, lo = got[8 * NODE : 8 * NODE + 64], got[8 * NODE + 64 :]
    qsum[...] = qown[...] + (hi.astype(F32) + lo.astype(F32))
    backward_own(FIRST, dense, bt, pos, got, (x1, x3))


def backward_own_last(pos, dense, bt, got, q, q1, q2, q3, qsum, x2, x0, held):
    ring_sum(pos[PX], (q, q1, q2, q3), qsum, held)
    backward_own(LAST, dense, bt, pos, got, (x2, x0))


def first_sum(pos, x0, r2, q, q1, q2, q3, t0, t1, t2, t3, qsum, held):
    ring_sum(pos[PZ], (q, q1, q2, q3), qsum, held)
    for d, out in enumerate((t0, t1, t2, t3)):
        at = slice(d * NODE, (d + 1) * NODE)
        out[...] = (x0[at] + r2[at].astype(F32)).astype(out.dtype)


def last_sum(t0, r1, r2, r3, out):
    s = t0[...]
    for r in (r1, r2, r3):
        s += r[...].astype(F32)
    out[...] = s.T.astype(BF16)


def weight_rows(pos, first, second, out):
    for r, i, p in ((first, 0, PY), (first, 64, PX1), (second, 0, PX3), (second, 64, PY2)):
        row = pl.multiple_of(pos[p] * 64, 64)
        out[pl.ds(row, 64), :] = r[i : i + 64] * (1.0 / NODE)


def send(v, axis, d, n=4):
    return lax.ppermute(v, axis, [(i, (i + d) % n) for i in range(n)])


def swap(v, axis, step):
    return lax.ppermute(v, axis, [(i, i ^ step) for i in range(4)])


def send_by_core(v, stage, d):
    pairs = []
    for z in range(4):
        for x in range(4):
            for core in range(2):
                if core == stage:
                    to = z, (x + d) % 4
                else:
                    to = (z + d) % 4, x
                pairs.append((z * 8 + x * 2 + core, to[0] * 8 + to[1] * 2 + core))
    return lax.ppermute(v, RING, pairs)


def body(features, cotangent, weight, tile_values, tile_rows, tile_cols, tile_count):
    tv, rows, cols, count = tile_values[0, 0], tile_rows, tile_cols, tile_count[0]
    z, x, core, y = (lax.axis_index(a) for a in ("z", "x", "core", "y"))
    places = [z, x, core] + [lax.rem(y + d, 4) for d in range(4)] + [y ^ 1, y ^ 3]
    pos = jnp.stack(places).astype(jnp.int32)
    tv, rows, cols = (pltpu.with_memory_space_constraint(v, pltpu.HBM) for v in (tv, rows, cols))

    near = {d: send_by_core(features, 0, -d) for d in (2, 1, 3)}
    near = jnp.concatenate([features] + [near[d] for d in (1, 2, 3)], axis=0)
    dense = call(dense_zeros, DENSE, [SSPEC], nbytes=16 * MIB)(pos)
    near, count, pos, dense = lax.optimization_barrier((near, count, pos, dense))
    far = [send_by_core(near, 1, -d) for d in FAR]
    near_other = send(near, "core", 1, 2)
    dense = call(
        dense_block,
        DENSE,
        [ASPEC, ASPEC, ASPEC, SSPEC, VSPEC],
        [pltpu.SMEM((1, 1, CAP), jnp.int32)] * 2 + [pltpu.SemaphoreType.DMA] * 3,
        nbytes=24 * MIB,
        aliases={4: 0},
    )(tv, rows, cols, count, in_vmem(dense))
    sums = shape((ROWS, FEAT), F32)
    dense, acc = dense_call(forward_near, [sums], dense, pos, near, near_other, cost=16 * MIB)
    far, acc = lax.optimization_barrier((far, acc))
    far = jnp.concatenate(far, axis=0)
    far_other = send(far, "core", 1, 2)
    dense, acc = dense_call(forward_own, [sums], dense, pos, far, acc)
    block, blockf = shape((NODE, FEAT), BF16), shape((NODE, FEAT), F32)

    def other_columns(dense, blocks, outs):
        kernel = functools.partial(forward_other, blocks)
        return dense_call(kernel, outs, dense, pos, far_other, acc)

    dense, s2, s1 = other_columns(dense, (PY2, PY1), [block, block])
    r2, r1 = send(s2, "y", 2), send(s1, "y", 1)
    dense, s3, own = other_columns(dense, (PY3, PY), [block, blockf])
    own = call(add_two, blockf, [VSPEC] * 3, nbytes=MIB // 2)(own, r1, r2)
    r3 = send(s3, "y", 3)

    packed = shape((NODE + 64, FEAT), BF16)
    activated, bt, q, m1, m2, m3 = call(
        middle,
        [block, block, shape((64, FEAT), F32), packed, packed, packed],
        [SSPEC] + [VSPEC] * 4,
        [pltpu.VMEM((FEAT, FEAT), F32)],
        flops=6 * FEAT**3,
        nbytes=MIB,
    )(pos, own, r3, weight, cotangent)
    r = {d: send(m, "y", d) for d, m in ((2, m2), (1, m1), (3, m3))}

    piece = shape((64, FEAT), F32)
    dense, other, bt, q = dense_call(
        backward_other_first,
        [shape((8 * NODE + 128, FEAT), BF16), shape((4, FEAT, NODE), BF16), piece],
        dense, pos, bt, r[1], r[2], r[3], q,
    )
    got_first = send(other, "core", 1, 2)
    dense, other = dense_call(
        backward_other_last, [shape((8 * NODE, FEAT), BF16)], dense, pos, bt
    )
    got_last = send(other, "core", 1, 2)
    long, longf = shape((4 * NODE, FEAT), BF16), shape((4 * NODE, FEAT), F32)

    held = [pltpu.VMEM((4, 64, FEAT), F32)]
    dense, q, x1, x3 = dense_call(
        backward_own_first, [piece, long, long], dense, pos, bt, got_first, q
    )
    along_x = [send(q, "x", d) for d in (1, 2, 3)]
    r1, r3 = send_by_core(x1, 0, 1), send_by_core(x3, 0, 3)
    dense, q, x2, x0 = dense_call(
        backward_own_last,
        [piece, long, longf],
        dense, pos, bt, got_last, q, *along_x,
        scratch=held,
    )
    r2 = send_by_core(x2, 0, 2)
    x0 = call(add_two, longf, [VSPEC] * 3, nbytes=MIB)(x0, r1, r3)
    t0, t1, t2, t3, q = call(
        first_sum,
        [blockf, block, block, block, piece],
        [SSPEC] + [VSPEC] * 6,
        held,
        nbytes=MIB,
    )(pos, x0, r2, q, *[send(q, "z", d) for d in (1, 2, 3)])
    r = {d: send_by_core(v, 1, d) for d, v in ((2, t2), (1, t1), (3, t3))}
    feature_grad = call(last_sum, block, [VSPEC] * 4, nbytes=MIB)(t0, r[1], r[2], r[3])
    first = jnp.concatenate([q, swap(q, "y", 1)], axis=0)
    weight_grad = call(
        weight_rows, shape((FEAT, FEAT), F32), [SSPEC, VSPEC, VSPEC], nbytes=MIB // 2
    )(pos, first, swap(first, "y", 3))
    return activated, weight_grad, feature_grad


def solution(mesh):
    parts = Mesh(mesh.devices.reshape(4, 4, 2, 4), ("z", "x", "core", "y"))
    return jax.shard_map(
        body,
        mesh=parts,
        in_specs=(
            P(("y",) + RING, None),
            P(RING + ("y",), None),
            P(),
            P(RING, "y", None, None, None),
            P(RING, "y", None),
            P(RING, "y", None),
            P(RING, "y"),
        ),
        out_specs=(P(RING + ("y",), None), P(), P(("y",) + RING, None)),
        check_vma=False,
    )
```

```python
import functools

import jax
import jax.numpy as jnp
from jax import lax
from jax.experimental import pallas as pl
from jax.experimental.pallas import tpu as pltpu
from jax.sharding import Mesh
from jax.sharding import PartitionSpec as P

F32 = jnp.float32
BF16 = jnp.bfloat16
TILE = 128
FEAT = 256
NODE = 256
HALF = 128
ROWS = 1024
NCT = 64
CAP = 384
MIB = 1 << 20
PZ, PX, PC, PY, PY1, PY2, PY3, PX1, PX3 = range(9)
RING = ("z", "x", "core")


def shape(s, dt):
    return jax.ShapeDtypeStruct(s, dt)


VSPEC = pl.BlockSpec(memory_space=pltpu.VMEM)
SSPEC = pl.BlockSpec(memory_space=pltpu.SMEM)
ASPEC = pl.BlockSpec(memory_space=pl.ANY)


def in_vmem(x):
    return pltpu.with_memory_space_constraint(x, pltpu.VMEM)


def call(kernel, outs, in_specs, scratch=(), flops=0, nbytes=0, limit=16, aliases=None):
    return pl.pallas_call(
        kernel,
        out_shape=outs,
        in_specs=in_specs,
        out_specs=jax.tree.map(lambda _: VSPEC, outs),
        scratch_shapes=list(scratch),
        input_output_aliases=aliases or {},
        cost_estimate=pl.CostEstimate(flops=flops, bytes_accessed=nbytes, transcendentals=0),
        compiler_params=pltpu.CompilerParams(vmem_limit_bytes=limit * MIB),
    )


DENSE = pltpu.VMEM((NCT, ROWS, TILE), BF16)
SIZE = NCT * ROWS * TILE


def dense_call(kernel, outs, dense, pos, *rest, scratch=(), cost=1000):
    n = 2 + len(rest)

    def wrapped(*refs):
        kernel(*refs[:n], *refs[n + 1 :])

    return call(
        wrapped,
        [DENSE] + outs,
        [SSPEC] + [VSPEC] * (n - 1),
        scratch,
        flops=cost,
        nbytes=cost,
        aliases={1: 0},
    )(pos, in_vmem(dense), *rest)


def dense_zeros(pos, dense):
    del pos

    @pl.loop(0, NCT)
    def _(c):
        dense[c] = jnp.zeros((ROWS, TILE), BF16)


def dense_block(tv, rows_in, cols_in, count, given, dense, rows, cols, sem, sem_rows, sem_cols):
    del given
    index_copies = (
        pltpu.make_async_copy(rows_in, rows, sem_rows),
        pltpu.make_async_copy(cols_in, cols, sem_cols),
    )
    for copy in index_copies:
        copy.start()
    for copy in index_copies:
        copy.wait()

    def tile(s):
        return pltpu.make_async_copy(
            tv.at[s],
            dense.at[cols[0, 0, s], pl.ds(pl.multiple_of(rows[0, 0, s] * TILE, TILE), TILE), :],
            sem,
        )

    def start(s, _):
        tile(s).start()
        return 0

    def wait(s, _):
        tile(s).wait()
        return 0

    lax.fori_loop(0, count[0], start, 0)
    lax.fori_loop(0, count[0], wait, 0)


def column_tile(pos, core, e, d):
    z = lax.rem(pos[PZ] + d + core * (e - d), 4)
    x = lax.rem(pos[PX] + e + core * (d - e), 4)
    return 2 * (z * 8 + x * 2 + core)


def tiles_of(dense, pos, core, d, rows):
    tiles = []
    for e in range(4):
        c = column_tile(pos, core, e, d)
        tiles += [jnp.concatenate([dense[c + i, r, :] for r in rows], axis=0) for i in range(2)]
    return jnp.concatenate(tiles, axis=1)


WHOLE = (slice(None),)


def forward_near(pos, dense, near, near_other, acc):
    core = pos[PC]
    acc[...] = jnp.dot(
        tiles_of(dense, pos, core, 0, WHOLE), near[...], preferred_element_type=F32
    ) + jnp.dot(
        tiles_of(dense, pos, 1 - core, 0, WHOLE), near_other[...], preferred_element_type=F32
    )


FAR = (1, 3, 2)


def far_sum(total, dense, pos, core, far, rows):
    for i, d in enumerate(FAR):
        rhs = far[i * ROWS : (i + 1) * ROWS]
        total += jnp.dot(tiles_of(dense, pos, core, d, rows), rhs, preferred_element_type=F32)
    return total


def forward_own(pos, dense, far, given, acc):
    acc[...] = far_sum(given[...], dense, pos, pos[PC], far, WHOLE)


def forward_other(blocks, pos, dense, far, given, *outs):
    rows = [pl.ds(pl.multiple_of(pos[b] * NODE, NODE), NODE) for b in blocks]
    total = jnp.concatenate([given[r, :] for r in rows], axis=0)
    total = far_sum(total, dense, pos, 1 - pos[PC], far, rows)
    for i, out in enumerate(outs):
        out[...] = total[i * NODE : (i + 1) * NODE].astype(out.dtype)


def add_one(own, r, out):
    out[...] = own[...] + r[...].astype(F32)


def add_two(own, r1, r2, out):
    out[...] = own[...] + r1[...].astype(F32) + r2[...].astype(F32)


def middle(pos, own, r3, w, cot, act, bt, q, m1, m2, m3, lg):
    agg = (own[...] + r3[...].astype(F32)).astype(BF16)
    pre = jnp.dot(agg, w[...], preferred_element_type=F32)
    sg = jax.nn.sigmoid(pre)
    act[...] = (pre * sg).astype(BF16)
    dz = (cot[...].astype(F32) * sg * (1.0 + pre * (1.0 - sg))).astype(BF16)
    back = lax.dot_general(w[...], dz, (((1,), (1,)), ((), ())), preferred_element_type=F32).astype(
        BF16
    )
    lg[...] = lax.dot_general(agg, dz, (((0,), (0,)), ((), ())), preferred_element_type=F32)
    bt[...] = back
    for p, out in ((PY, q), (PY1, m1), (PY2, m2), (PY3, m3)):
        piece = lg[pl.ds(pl.multiple_of(pos[p] * 64, 64), 64), :]
        if p == PY:
            out[...] = piece
        else:
            out[:NODE] = back
            out[NODE:] = piece.astype(BF16)


FIRST, LAST = (2, 0), (1, 3)


def back_all(bt):
    return jnp.concatenate([bt[0], bt[1], bt[2], bt[3]], axis=1)


def backward_block(dense, lhs, pos, core, e, d):
    c = column_tile(pos, core, e, d)
    rhs = jnp.concatenate([dense[c], dense[c + 1]], axis=1)
    return jnp.dot(lhs, rhs, preferred_element_type=F32)


def backward_other(distances, dense, lhs, pos, out):
    for k, e in enumerate(distances):
        for d in range(4):
            i = (k * 4 + d) * NODE
            out[i : i + NODE] = backward_block(dense, lhs, pos, 1 - pos[PC], e, d).astype(BF16)


def two_parts(v):
    hi = v.astype(BF16)
    return hi, (v - hi.astype(F32)).astype(BF16)


def backward_other_first(pos, dense, own, r1, r2, r3, q, out, bt, qown):
    y = pos[PY]
    bt[y] = own[...]
    total = q[...]
    for d, r in ((1, r1), (2, r2), (3, r3)):
        bt[lax.rem(y + 4 - d, 4)] = r[:NODE]
        total += r[NODE:].astype(F32)
    hi, lo = two_parts(total)
    qown[...] = hi.astype(F32) + lo.astype(F32)
    out[8 * NODE : 8 * NODE + 64] = hi
    out[8 * NODE + 64 :] = lo
    backward_other(FIRST, dense, back_all(bt), pos, out)


def backward_other_last(pos, dense, bt, out):
    backward_other(LAST, dense, back_all(bt), pos, out)


def backward_own(distances, dense, bt, pos, got, outs):
    lhs = back_all(bt)
    for k, (e, out) in enumerate(zip(distances, outs, strict=True)):
        for d in range(4):
            i = (k * 4 + d) * NODE
            g = backward_block(dense, lhs, pos, pos[PC], e, d) + got[i : i + NODE].astype(F32)
            out[d * NODE : (d + 1) * NODE] = g.astype(out.dtype)


def ring_sum(place, terms, out, held):
    for d, term in enumerate(terms):
        held[lax.rem(place + 4 - d, 4)] = term[...].astype(F32)
    out[...] = ((held[0] + held[1]) + (held[2] + held[3])).astype(out.dtype)


def backward_own_first(pos, dense, bt, got, qown, qsum, x2, x0):
    hi, lo = got[8 * NODE : 8 * NODE + 64], got[8 * NODE + 64 :]
    qsum[...] = (qown[...] + (hi.astype(F32) + lo.astype(F32))).astype(BF16)
    backward_own(FIRST, dense, bt, pos, got, (x2, x0))


def backward_own_last(pos, dense, bt, got, q, q1, q2, q3, qsum, x1, x3, held):
    ring_sum(pos[PX], (q, q1, q2, q3), qsum, held)
    backward_own(LAST, dense, bt, pos, got, (x1, x3))


def first_sum(pos, x0, r1, r3, q, q1, q2, q3, t0, t1, t2, t3, qsum, held):
    ring_sum(pos[PZ], (q, q1, q2, q3), qsum, held)
    for d, out in enumerate((t0, t1, t2, t3)):
        at = slice(d * NODE, (d + 1) * NODE)
        out[...] = (x0[at] + r1[at].astype(F32) + r3[at].astype(F32)).astype(out.dtype)


def last_sum(pos, t0, r1, r2, r3, first, second, out, grad):
    s = t0[...]
    for r in (r1, r2, r3):
        s += r[...].astype(F32)
    out[...] = s.T.astype(BF16)
    for r, i, p in ((first, 0, PY), (first, 64, PX1), (second, 0, PX3), (second, 64, PY2)):
        row = pl.multiple_of(pos[p] * 64, 64)
        grad[pl.ds(row, 64), :] = r[i : i + 64] * (1.0 / NODE)


def send(v, axis, d, n=4):
    return lax.ppermute(v, axis, [(i, (i + d) % n) for i in range(n)])


def swap(v, axis, step):
    return lax.ppermute(v, axis, [(i, i ^ step) for i in range(4)])


def send_by_core(v, stage, d):
    pairs = []
    for z in range(4):
        for x in range(4):
            for core in range(2):
                if core == stage:
                    to = z, (x + d) % 4
                else:
                    to = (z + d) % 4, x
                pairs.append((z * 8 + x * 2 + core, to[0] * 8 + to[1] * 2 + core))
    return lax.ppermute(v, RING, pairs)


def body(features, cotangent, weight, tile_values, tile_rows, tile_cols, tile_count):
    tv, rows, cols, count = tile_values[0, 0], tile_rows, tile_cols, tile_count[0]
    z, x, core, y = (lax.axis_index(a) for a in ("z", "x", "core", "y"))
    places = [z, x, core] + [lax.rem(y + d, 4) for d in range(4)] + [y ^ 1, y ^ 3]
    pos = jnp.stack(places).astype(jnp.int32)
    tv, rows, cols = (pltpu.with_memory_space_constraint(v, pltpu.HBM) for v in (tv, rows, cols))

    near = {d: send_by_core(features, 0, -d) for d in (2, 1, 3)}
    near = jnp.concatenate([features] + [near[d] for d in (1, 2, 3)], axis=0)
    dense = call(dense_zeros, DENSE, [SSPEC], nbytes=16 * MIB)(pos)
    near, count, pos, dense = lax.optimization_barrier((near, count, pos, dense))
    far = [send_by_core(near, 1, -d) for d in FAR]
    near_other = send(near, "core", 1, 2)
    dense = call(
        dense_block,
        DENSE,
        [ASPEC, ASPEC, ASPEC, SSPEC, VSPEC],
        [pltpu.SMEM((1, 1, CAP), jnp.int32)] * 2 + [pltpu.SemaphoreType.DMA] * 3,
        nbytes=24 * MIB,
        aliases={4: 0},
    )(tv, rows, cols, count, in_vmem(dense))
    sums = shape((ROWS, FEAT), F32)
    dense, acc = dense_call(forward_near, [sums], dense, pos, near, near_other, cost=16 * MIB)
    far, acc = lax.optimization_barrier((far, acc))
    far = jnp.concatenate(far, axis=0)
    far_other = send(far, "core", 1, 2)
    dense, acc = dense_call(forward_own, [sums], dense, pos, far, acc)
    block, blockf = shape((NODE, FEAT), BF16), shape((NODE, FEAT), F32)

    def other_columns(dense, blocks, outs):
        kernel = functools.partial(forward_other, blocks)
        return dense_call(kernel, outs, dense, pos, far_other, acc)

    dense, s2, s1 = other_columns(dense, (PY2, PY1), [block, block])
    r2, r1 = send(s2, "y", 2), send(s1, "y", 1)
    dense, s3, own = other_columns(dense, (PY3, PY), [block, blockf])
    own = call(add_two, blockf, [VSPEC] * 3, nbytes=MIB // 2)(own, r1, r2)
    r3 = send(s3, "y", 3)

    packed = shape((NODE + 64, FEAT), BF16)
    activated, bt, q, m1, m2, m3 = call(
        middle,
        [block, block, shape((64, FEAT), F32), packed, packed, packed],
        [SSPEC] + [VSPEC] * 4,
        [pltpu.VMEM((FEAT, FEAT), F32)],
        flops=6 * FEAT**3,
        nbytes=MIB,
    )(pos, own, r3, weight, cotangent)
    r = {d: send(m, "y", d) for d, m in ((2, m2), (1, m1), (3, m3))}

    piece = shape((64, FEAT), F32)
    dense, other, bt, q = dense_call(
        backward_other_first,
        [shape((8 * NODE + 128, FEAT), BF16), shape((4, FEAT, NODE), BF16), piece],
        dense, pos, bt, r[1], r[2], r[3], q,
    )
    got_first = send(other, "core", 1, 2)
    dense, other = dense_call(
        backward_other_last, [shape((8 * NODE, FEAT), BF16)], dense, pos, bt
    )
    got_last = send(other, "core", 1, 2)
    long, longf = shape((4 * NODE, FEAT), BF16), shape((4 * NODE, FEAT), F32)

    held = [pltpu.VMEM((4, 64, FEAT), F32)]
    rounded = shape((64, FEAT), BF16)
    dense, q, x2, x0 = dense_call(
        backward_own_first, [rounded, long, longf], dense, pos, bt, got_first, q
    )
    along_x = [send(q, "x", d) for d in (1, 2, 3)]
    r2 = send_by_core(x2, 0, 2)
    dense, q, x1, x3 = dense_call(
        backward_own_last,
        [rounded, long, long],
        dense, pos, bt, got_last, q, *along_x,
        scratch=held,
    )
    r1, r3 = send_by_core(x1, 0, 1), send_by_core(x3, 0, 3)
    x0 = call(add_one, longf, [VSPEC] * 2, nbytes=MIB)(x0, r2)
    t0, t1, t2, t3, q = call(
        first_sum,
        [blockf, block, block, block, piece],
        [SSPEC] + [VSPEC] * 7,
        held,
        nbytes=MIB,
    )(pos, x0, r1, r3, q, *[send(q, "z", d) for d in (1, 2, 3)])
    r = {d: send_by_core(v, 1, d) for d, v in ((2, t2), (1, t1), (3, t3))}
    first = jnp.concatenate([q, swap(q, "y", 1)], axis=0)
    feature_grad, weight_grad = call(
        last_sum, [block, shape((FEAT, FEAT), F32)], [SSPEC] + [VSPEC] * 6, nbytes=MIB
    )(pos, t0, r[1], r[2], r[3], first, swap(first, "y", 3))
    return activated, weight_grad, feature_grad


def solution(mesh):
    parts = Mesh(mesh.devices.reshape(4, 4, 2, 4), ("z", "x", "core", "y"))
    return jax.shard_map(
        body,
        mesh=parts,
        in_specs=(
            P(("y",) + RING, None),
            P(RING + ("y",), None),
            P(),
            P(RING, "y", None, None, None),
            P(RING, "y", None),
            P(RING, "y", None),
            P(RING, "y"),
        ),
        out_specs=(P(RING + ("y",), None), P(), P(("y",) + RING, None)),
        check_vma=False,
    )
```

```python
import functools

import jax
import jax.numpy as jnp
from jax import lax
from jax.experimental import pallas as pl
from jax.experimental.pallas import tpu as pltpu
from jax.sharding import Mesh
from jax.sharding import PartitionSpec as P

F32 = jnp.float32
BF16 = jnp.bfloat16
TILE = 128
FEAT = 256
NODE = 256
HALF = 128
ROWS = 1024
NCT = 64
CAP = 384
MIB = 1 << 20
PZ, PX, PC, PY, PY1, PY2, PY3, PX1, PX3 = range(9)
RING = ("z", "x", "core")


def shape(s, dt):
    return jax.ShapeDtypeStruct(s, dt)


VSPEC = pl.BlockSpec(memory_space=pltpu.VMEM)
SSPEC = pl.BlockSpec(memory_space=pltpu.SMEM)
ASPEC = pl.BlockSpec(memory_space=pl.ANY)


def in_vmem(x):
    return pltpu.with_memory_space_constraint(x, pltpu.VMEM)


def call(kernel, outs, in_specs, scratch=(), flops=0, nbytes=0, limit=16, aliases=None):
    return pl.pallas_call(
        kernel,
        out_shape=outs,
        in_specs=in_specs,
        out_specs=jax.tree.map(lambda _: VSPEC, outs),
        scratch_shapes=list(scratch),
        input_output_aliases=aliases or {},
        cost_estimate=pl.CostEstimate(flops=flops, bytes_accessed=nbytes, transcendentals=0),
        compiler_params=pltpu.CompilerParams(vmem_limit_bytes=limit * MIB),
    )


DENSE = pltpu.VMEM((NCT, ROWS, TILE), BF16)
SIZE = NCT * ROWS * TILE


def dense_call(kernel, outs, dense, pos, *rest, scratch=(), cost=1000):
    n = 2 + len(rest)

    def wrapped(*refs):
        kernel(*refs[:n], *refs[n + 1 :])

    return call(
        wrapped,
        [DENSE] + outs,
        [SSPEC] + [VSPEC] * (n - 1),
        scratch,
        flops=cost,
        nbytes=cost,
        aliases={1: 0},
    )(pos, in_vmem(dense), *rest)


def dense_zeros(pos, dense):
    del pos

    @pl.loop(0, NCT)
    def _(c):
        dense[c] = jnp.zeros((ROWS, TILE), BF16)


def dense_block(tv, rows_in, cols_in, count, given, dense, rows, cols, sem, sem_rows, sem_cols):
    del given
    index_copies = (
        pltpu.make_async_copy(rows_in, rows, sem_rows),
        pltpu.make_async_copy(cols_in, cols, sem_cols),
    )
    for copy in index_copies:
        copy.start()
    for copy in index_copies:
        copy.wait()

    def tile(s):
        return pltpu.make_async_copy(
            tv.at[s],
            dense.at[cols[0, 0, s], pl.ds(pl.multiple_of(rows[0, 0, s] * TILE, TILE), TILE), :],
            sem,
        )

    def start(s, _):
        tile(s).start()
        return 0

    def wait(s, _):
        tile(s).wait()
        return 0

    lax.fori_loop(0, count[0], start, 0)
    lax.fori_loop(0, count[0], wait, 0)


def column_tile(pos, core, e, d):
    z = lax.rem(pos[PZ] + d + core * (e - d), 4)
    x = lax.rem(pos[PX] + e + core * (d - e), 4)
    return 2 * (z * 8 + x * 2 + core)


def tiles_of(dense, pos, core, d, rows):
    tiles = []
    for e in range(4):
        c = column_tile(pos, core, e, d)
        tiles += [jnp.concatenate([dense[c + i, r, :] for r in rows], axis=0) for i in range(2)]
    return jnp.concatenate(tiles, axis=1)


WHOLE = (slice(None),)


def near_sum(dense, pos, core, near):
    return jnp.dot(tiles_of(dense, pos, core, 0, WHOLE), near[...], preferred_element_type=F32)


def forward_near(pos, dense, near, acc):
    acc[...] = near_sum(dense, pos, pos[PC], near)


FAR = (1, 3, 2)


def far_sum(total, dense, pos, core, far, rows):
    for i, d in enumerate(FAR):
        rhs = far[i * ROWS : (i + 1) * ROWS]
        total += jnp.dot(tiles_of(dense, pos, core, d, rows), rhs, preferred_element_type=F32)
    return total


def forward_own(pos, dense, far, near_other, given, acc):
    total = given[...] + near_sum(dense, pos, 1 - pos[PC], near_other)
    acc[...] = far_sum(total, dense, pos, pos[PC], far, WHOLE)


def forward_other(blocks, pos, dense, far, given, *outs):
    rows = [pl.ds(pl.multiple_of(pos[b] * NODE, NODE), NODE) for b in blocks]
    total = jnp.concatenate([given[r, :] for r in rows], axis=0)
    total = far_sum(total, dense, pos, 1 - pos[PC], far, rows)
    for i, out in enumerate(outs):
        out[...] = total[i * NODE : (i + 1) * NODE].astype(out.dtype)


def add_one(own, r, out):
    out[...] = own[...] + r[...].astype(F32)


def add_two(own, r1, r2, out):
    out[...] = own[...] + r1[...].astype(F32) + r2[...].astype(F32)


def middle(pos, own, r3, w, cot, act, bt, q, m1, m2, m3, lg):
    agg = (own[...] + r3[...].astype(F32)).astype(BF16)
    pre = jnp.dot(agg, w[...], preferred_element_type=F32)
    sg = jax.nn.sigmoid(pre)
    act[...] = (pre * sg).astype(BF16)
    dz = (cot[...].astype(F32) * sg * (1.0 + pre * (1.0 - sg))).astype(BF16)
    back = lax.dot_general(w[...], dz, (((1,), (1,)), ((), ())), preferred_element_type=F32).astype(
        BF16
    )
    lg[...] = lax.dot_general(agg, dz, (((0,), (0,)), ((), ())), preferred_element_type=F32)
    bt[...] = back
    for p, out in ((PY, q), (PY1, m1), (PY2, m2), (PY3, m3)):
        piece = lg[pl.ds(pl.multiple_of(pos[p] * 64, 64), 64), :]
        if p == PY:
            out[...] = piece
        else:
            out[:NODE] = back
            out[NODE:] = piece.astype(BF16)


FIRST, LAST = (2, 0), (1, 3)


def back_all(bt):
    return jnp.concatenate([bt[0], bt[1], bt[2], bt[3]], axis=1)


def backward_block(dense, lhs, pos, core, e, d):
    c = column_tile(pos, core, e, d)
    rhs = jnp.concatenate([dense[c], dense[c + 1]], axis=1)
    return jnp.dot(lhs, rhs, preferred_element_type=F32)


def backward_other(distances, dense, lhs, pos, out):
    for k, e in enumerate(distances):
        for d in range(4):
            i = (k * 4 + d) * NODE
            out[i : i + NODE] = backward_block(dense, lhs, pos, 1 - pos[PC], e, d).astype(BF16)


def two_parts(v):
    hi = v.astype(BF16)
    return hi, (v - hi.astype(F32)).astype(BF16)


def backward_other_first(pos, dense, own, r1, r2, r3, q, out, bt, qown):
    y = pos[PY]
    bt[y] = own[...]
    total = q[...]
    for d, r in ((1, r1), (2, r2), (3, r3)):
        bt[lax.rem(y + 4 - d, 4)] = r[:NODE]
        total += r[NODE:].astype(F32)
    hi, lo = two_parts(total)
    qown[...] = hi.astype(F32) + lo.astype(F32)
    out[8 * NODE : 8 * NODE + 64] = hi
    out[8 * NODE + 64 :] = lo
    backward_other(FIRST, dense, back_all(bt), pos, out)


def backward_other_last(pos, dense, bt, out):
    backward_other(LAST, dense, back_all(bt), pos, out)


def backward_own(distances, dense, bt, pos, got, outs):
    lhs = back_all(bt)
    for k, (e, out) in enumerate(zip(distances, outs, strict=True)):
        for d in range(4):
            i = (k * 4 + d) * NODE
            g = backward_block(dense, lhs, pos, pos[PC], e, d) + got[i : i + NODE].astype(F32)
            out[d * NODE : (d + 1) * NODE] = g.astype(out.dtype)


def ring_sum(place, terms, out, held):
    for d, term in enumerate(terms):
        held[lax.rem(place + 4 - d, 4)] = term[...].astype(F32)
    out[...] = ((held[0] + held[1]) + (held[2] + held[3])).astype(out.dtype)


def backward_own_first(pos, dense, bt, got, qown, qsum, x2, x0):
    hi, lo = got[8 * NODE : 8 * NODE + 64], got[8 * NODE + 64 :]
    qsum[...] = (qown[...] + (hi.astype(F32) + lo.astype(F32))).astype(BF16)
    backward_own(FIRST, dense, bt, pos, got, (x2, x0))


def backward_own_last(pos, dense, bt, got, q, q1, q2, q3, qsum, x1, x3, held):
    ring_sum(pos[PX], (q, q1, q2, q3), qsum, held)
    backward_own(LAST, dense, bt, pos, got, (x1, x3))


def first_sum(pos, x0, r1, r3, q, q1, q2, q3, t0, t1, t2, t3, qsum, held):
    ring_sum(pos[PZ], (q, q1, q2, q3), qsum, held)
    for d, out in enumerate((t0, t1, t2, t3)):
        at = slice(d * NODE, (d + 1) * NODE)
        out[...] = (x0[at] + r1[at].astype(F32) + r3[at].astype(F32)).astype(out.dtype)


def last_sum(pos, t0, r1, r2, r3, first, second, out, grad):
    s = t0[...]
    for r in (r1, r2, r3):
        s += r[...].astype(F32)
    out[...] = s.T.astype(BF16)
    for r, i, p in ((first, 0, PY), (first, 64, PX1), (second, 0, PX3), (second, 64, PY2)):
        row = pl.multiple_of(pos[p] * 64, 64)
        grad[pl.ds(row, 64), :] = r[i : i + 64] * (1.0 / NODE)


def send(v, axis, d, n=4):
    return lax.ppermute(v, axis, [(i, (i + d) % n) for i in range(n)])


def swap(v, axis, step):
    return lax.ppermute(v, axis, [(i, i ^ step) for i in range(4)])


def send_by_core(v, stage, d):
    pairs = []
    for z in range(4):
        for x in range(4):
            for core in range(2):
                if core == stage:
                    to = z, (x + d) % 4
                else:
                    to = (z + d) % 4, x
                pairs.append((z * 8 + x * 2 + core, to[0] * 8 + to[1] * 2 + core))
    return lax.ppermute(v, RING, pairs)


def body(features, cotangent, weight, tile_values, tile_rows, tile_cols, tile_count):
    tv, rows, cols, count = tile_values[0, 0], tile_rows, tile_cols, tile_count[0]
    z, x, core, y = (lax.axis_index(a) for a in ("z", "x", "core", "y"))
    places = [z, x, core] + [lax.rem(y + d, 4) for d in range(4)] + [y ^ 1, y ^ 3]
    pos = jnp.stack(places).astype(jnp.int32)
    tv, rows, cols = (pltpu.with_memory_space_constraint(v, pltpu.HBM) for v in (tv, rows, cols))

    near = {d: send_by_core(features, 0, -d) for d in (2, 1, 3)}
    near = jnp.concatenate([features] + [near[d] for d in (1, 2, 3)], axis=0)
    dense = call(dense_zeros, DENSE, [SSPEC], nbytes=16 * MIB)(pos)
    near, count, pos, dense = lax.optimization_barrier((near, count, pos, dense))
    far = [send_by_core(near, 1, -d) for d in FAR]
    near_other = send(near, "core", 1, 2)
    dense = call(
        dense_block,
        DENSE,
        [ASPEC, ASPEC, ASPEC, SSPEC, VSPEC],
        [pltpu.SMEM((1, 1, CAP), jnp.int32)] * 2 + [pltpu.SemaphoreType.DMA] * 3,
        nbytes=24 * MIB,
        aliases={4: 0},
    )(tv, rows, cols, count, in_vmem(dense))
    sums = shape((ROWS, FEAT), F32)
    dense, acc = dense_call(forward_near, [sums], dense, pos, near, cost=16 * MIB)
    far, acc, near_other = lax.optimization_barrier((far, acc, near_other))
    far = jnp.concatenate(far, axis=0)
    far_other = send(far, "core", 1, 2)
    dense, acc = dense_call(forward_own, [sums], dense, pos, far, near_other, acc)
    block, blockf = shape((NODE, FEAT), BF16), shape((NODE, FEAT), F32)

    def other_columns(dense, blocks, outs):
        kernel = functools.partial(forward_other, blocks)
        return dense_call(kernel, outs, dense, pos, far_other, acc)

    dense, s2, s1 = other_columns(dense, (PY2, PY1), [block, block])
    r2, r1 = send(s2, "y", 2), send(s1, "y", 1)
    dense, s3, own = other_columns(dense, (PY3, PY), [block, blockf])
    own = call(add_two, blockf, [VSPEC] * 3, nbytes=MIB // 2)(own, r1, r2)
    r3 = send(s3, "y", 3)

    packed = shape((NODE + 64, FEAT), BF16)
    activated, bt, q, m1, m2, m3 = call(
        middle,
        [block, block, shape((64, FEAT), F32), packed, packed, packed],
        [SSPEC] + [VSPEC] * 4,
        [pltpu.VMEM((FEAT, FEAT), F32)],
        flops=6 * FEAT**3,
        nbytes=MIB,
    )(pos, own, r3, weight, cotangent)
    r = {d: send(m, "y", d) for d, m in ((2, m2), (1, m1), (3, m3))}

    piece = shape((64, FEAT), F32)
    dense, other, bt, q = dense_call(
        backward_other_first,
        [shape((8 * NODE + 128, FEAT), BF16), shape((4, FEAT, NODE), BF16), piece],
        dense, pos, bt, r[1], r[2], r[3], q,
    )
    got_first = send(other, "core", 1, 2)
    dense, other = dense_call(
        backward_other_last, [shape((8 * NODE, FEAT), BF16)], dense, pos, bt
    )
    got_last = send(other, "core", 1, 2)
    long, longf = shape((4 * NODE, FEAT), BF16), shape((4 * NODE, FEAT), F32)

    held = [pltpu.VMEM((4, 64, FEAT), F32)]
    rounded = shape((64, FEAT), BF16)
    dense, q, x2, x0 = dense_call(
        backward_own_first, [rounded, long, longf], dense, pos, bt, got_first, q
    )
    along_x = [send(q, "x", d) for d in (1, 2, 3)]
    r2 = send_by_core(x2, 0, 2)
    dense, q, x1, x3 = dense_call(
        backward_own_last,
        [rounded, long, long],
        dense, pos, bt, got_last, q, *along_x,
        scratch=held,
    )
    r1, r3 = send_by_core(x1, 0, 1), send_by_core(x3, 0, 3)
    x0 = call(add_one, longf, [VSPEC] * 2, nbytes=MIB)(x0, r2)
    t0, t1, t2, t3, q = call(
        first_sum,
        [blockf, block, block, block, piece],
        [SSPEC] + [VSPEC] * 7,
        held,
        nbytes=MIB,
    )(pos, x0, r1, r3, q, *[send(q, "z", d) for d in (1, 2, 3)])
    r = {d: send_by_core(v, 1, d) for d, v in ((2, t2), (1, t1), (3, t3))}
    first = jnp.concatenate([q, swap(q, "y", 1)], axis=0)
    feature_grad, weight_grad = call(
        last_sum, [block, shape((FEAT, FEAT), F32)], [SSPEC] + [VSPEC] * 6, nbytes=MIB
    )(pos, t0, r[1], r[2], r[3], first, swap(first, "y", 3))
    return activated, weight_grad, feature_grad


def solution(mesh):
    parts = Mesh(mesh.devices.reshape(4, 4, 2, 4), ("z", "x", "core", "y"))
    return jax.shard_map(
        body,
        mesh=parts,
        in_specs=(
            P(("y",) + RING, None),
            P(RING + ("y",), None),
            P(),
            P(RING, "y", None, None, None),
            P(RING, "y", None),
            P(RING, "y", None),
            P(RING, "y"),
        ),
        out_specs=(P(RING + ("y",), None), P(), P(("y",) + RING, None)),
        check_vma=False,
    )
```
